128 devices in a mesh: dp: 8 (over y, core), tm: 16 (over z, x).
Axes of the slice: x: 4, y: 4, z: 4, core: 2. Of those that a mesh axis runs over, the one named last changes fastest.
Arguments:
- tokens: bfloat16 [8, 16, 384, 2048], P('dp', 'tm'), may hold values from -6 to 6
- cotangent: bfloat16 [8, 16, 384, 2048], P('dp', 'tm'), may hold values from -6 to 6
- norm_gain: bfloat16 [2048], replicated, may hold values from 0.25 to 1.75
- w_query: bfloat16 [2048, 1024], P(('dp', 'tm'))
- w_key: bfloat16 [2048, 1024], P(('dp', 'tm'))
- w_value: bfloat16 [2048, 1024], P(('dp', 'tm')), may hold values from -0.125 to 0.125
- w_out: bfloat16 [1024, 2048], P(('dp', 'tm')), may hold values from -0.1875 to 0.1875
Outputs:
- mixed: bfloat16 [8, 16, 384, 2048], P('dp', 'tm')
- grad_tokens: bfloat16 [8, 16, 384, 2048], P('dp', 'tm')
- grad_gain: float32 [2048], P(('dp', 'tm'))
- grad_query: float32 [2048, 1024], P(('dp', 'tm'))
- grad_key: float32 [2048, 1024], P(('dp', 'tm'))
- grad_value: float32 [2048, 1024], P(('dp', 'tm'))
- grad_out: float32 [1024, 2048], P(('dp', 'tm'))
The draws below stay inside these ranges and needn't reach their ends.
All inputs are finite; a program needn't handle non-finite values.
Results may differ from the reference program's by a relative error of at most 0.024.
The reference program's roundings to bfloat16 on the way (of `normed`, `query`, `upstream`, `prob_b`, `attended`, `dscore_b`, `dquery` and `terms`) count: a program that leaves them out, or rounds other values in their place, can miss the bound.
Values may be sent and summed in bfloat16 or wider, within the bound.
A program may use at most 128 MiB of HBM per device.

```python
import jax
import jax.numpy as jnp
from jax import lax

D = 2048
HEADS = 8
HEAD = 128
PATCH = 384
HD = 1024
CLIPS = 8
FRAMES = 16


def query_base(key):
    return jax.random.normal(jax.random.fold_in(key, 11), (D, HEADS * HEAD), jnp.float32) * D ** (-0.5)


def draw_w_query(key, part):
    shared = query_base(key)
    return shared.astype(jnp.bfloat16)


def draw_w_key(key, part):
    key = jax.random.fold_in(key, 3)
    first = jax.random.fold_in(key, 0)
    own = jax.random.normal(first, (D, HEADS * HEAD), jnp.float32) * D ** (-0.5)
    return own.astype(jnp.bfloat16)


def draw_tokens(key, part):
    key = jax.random.fold_in(key, 1)
    first = jax.random.fold_in(key, 0)
    base = jax.random.normal(first, (CLIPS, FRAMES, PATCH, D), jnp.float32)
    return jnp.clip(base, -6.0, 6.0).astype(jnp.bfloat16)


def steps_of(own_key, dims, shards, low, high):
    def one(position, parts):
        steps = jax.random.uniform(jax.random.fold_in(jax.random.fold_in(own_key, 6), position), (parts,), jnp.float32, low / len(shards), high / len(shards))
        return jnp.repeat(jnp.exp(steps), dims[position] // parts).reshape((-1,) + (1,) * (len(dims) - position - 1))

    factor_of = one(*shards[0])
    for cut in shards[1:]:
        factor_of = factor_of * one(*cut)
    return factor_of


def centred(stream_key, shape, spread, limit, cuts=(), kind=jnp.bfloat16):
    values = spread * jax.random.normal(stream_key, shape, jnp.float32)
    if cuts:
        values = values * steps_of(stream_key, shape, cuts, -0.22, 0.18)
    return jnp.clip(values, -limit, limit).astype(kind)


def setup_inputs(seed: int = 0) -> dict:
    key_of = jax.random.split(jax.random.key(seed), 8)
    tokens = draw_tokens(jax.random.fold_in(key_of[7], 71), 0)
    cotangent = centred(key_of[1], (CLIPS, FRAMES, PATCH, D), 1.0, 6.0, ((0, 8), (1, 16)))
    norm_gain = jnp.clip(1.0 + 0.15 * jax.random.normal(key_of[2], (D,), jnp.float32), 0.25, 1.75).astype(jnp.bfloat16)
    w_query = draw_w_query(jax.random.fold_in(key_of[7], 71), 0)
    w_key = draw_w_key(jax.random.fold_in(key_of[7], 71), 0)
    w_value = centred(key_of[5], (D, HD), D ** -0.5, 0.125, ((0, 128),))
    w_out = centred(key_of[6], (HD, D), HD ** -0.5, 0.1875, ((0, 128),))
    return dict(tokens=tokens, cotangent=cotangent, norm_gain=norm_gain, w_query=w_query, w_key=w_key, w_value=w_value, w_out=w_out)


def norm_parts(tokens, norm_gain):
    values = tokens.astype(jnp.float32)
    centre = lax.optimization_barrier(jnp.mean(values, axis=-1, keepdims=True))
    centered = values - centre
    variance = lax.optimization_barrier(jnp.mean(centered * centered, axis=-1, keepdims=True))
    inverse = lax.rsqrt(variance + 1e-05)
    scaled = centered * inverse
    normed = (scaled * norm_gain.astype(jnp.float32)).astype(jnp.bfloat16)
    return (scaled, inverse, normed)

def split_heads(array):
    return array.reshape(array.shape[:3] + (HEADS, HEAD)).astype(jnp.float32)

def attend(query, keys, values, upstream):
    shape = query.shape
    factor = HEAD ** (-0.5)
    q_heads = split_heads(query)
    k_heads = split_heads(keys)
    v_heads = split_heads(values)
    d_heads = split_heads(upstream)
    scores = jnp.einsum('cfphe,cgphe->cphfg', q_heads, k_heads) * factor
    later = lax.broadcasted_iota(jnp.int32, (shape[1], shape[1]), 0)
    earlier = lax.broadcasted_iota(jnp.int32, (shape[1], shape[1]), 1)
    scores = jnp.where(earlier <= later, scores, -1e+30)
    highest = lax.optimization_barrier(jnp.max(scores, axis=-1, keepdims=True))
    weights = jnp.exp(scores - highest)
    prob = weights / lax.optimization_barrier(jnp.sum(weights, axis=-1, keepdims=True))
    prob_b = prob.astype(jnp.bfloat16).astype(jnp.float32)
    attended = jnp.einsum('cphfg,cgphe->cfphe', prob_b, v_heads).astype(jnp.bfloat16).reshape(shape)
    dprob = jnp.einsum('cfphe,cgphe->cphfg', d_heads, v_heads)
    dscore = prob * (dprob - lax.optimization_barrier(jnp.sum(prob * dprob, axis=-1, keepdims=True)))
    dscore_b = dscore.astype(jnp.bfloat16).astype(jnp.float32)
    dquery = (jnp.einsum('cphfg,cgphe->cfphe', dscore_b, k_heads) * factor).astype(jnp.bfloat16).reshape(shape)
    dkeys = (jnp.einsum('cphfg,cfphe->cgphe', dscore_b, q_heads) * factor).astype(jnp.bfloat16).reshape(shape)
    dvalues = jnp.einsum('cphfg,cfphe->cgphe', prob_b, d_heads).astype(jnp.bfloat16).reshape(shape)
    return (attended, dquery, dkeys, dvalues)

def round_trip(term):
    return lax.optimization_barrier(term.astype(jnp.bfloat16)).astype(jnp.float32)

def reference(tokens, cotangent, norm_gain, w_query, w_key, w_value, w_out):
    scaled, inverse, normed = norm_parts(tokens, norm_gain)
    query = jnp.dot(normed, w_query, preferred_element_type=jnp.float32).astype(jnp.bfloat16)
    keys = jnp.dot(normed, w_key, preferred_element_type=jnp.float32).astype(jnp.bfloat16)
    values = jnp.dot(normed, w_value, preferred_element_type=jnp.float32).astype(jnp.bfloat16)
    upstream = jnp.dot(cotangent, w_out.T, preferred_element_type=jnp.float32).astype(jnp.bfloat16)
    attended, dquery, dkeys, dvalues = attend(query, keys, values, upstream)
    mixed = (tokens.astype(jnp.float32) + jnp.dot(attended, w_out, preferred_element_type=jnp.float32)).astype(jnp.bfloat16)
    dnormed = jnp.dot(dquery, w_query.T, preferred_element_type=jnp.float32)
    dnormed = dnormed + jnp.dot(dkeys, w_key.T, preferred_element_type=jnp.float32)
    dnormed = dnormed + jnp.dot(dvalues, w_value.T, preferred_element_type=jnp.float32)
    dscaled = dnormed * norm_gain.astype(jnp.float32)
    first_mean = lax.optimization_barrier(jnp.mean(dscaled, axis=-1, keepdims=True))
    second_mean = lax.optimization_barrier(jnp.mean(dscaled * scaled, axis=-1, keepdims=True))
    grad_tokens = (inverse * (dscaled - first_mean - scaled * second_mean) + cotangent.astype(jnp.float32)).astype(jnp.bfloat16)
    blocks = CLIPS * FRAMES

    def flat(array):
        return array.reshape((blocks,) + array.shape[2:])
    gain_terms = dnormed * scaled

    def accumulate(carry, pieces):
        normed_rows, dq_rows, dk_rows, dv_rows, att_rows, cot_rows, gain_rows = pieces
        terms = (jnp.dot(normed_rows.T, dq_rows, preferred_element_type=jnp.float32), jnp.dot(normed_rows.T, dk_rows, preferred_element_type=jnp.float32), jnp.dot(normed_rows.T, dv_rows, preferred_element_type=jnp.float32), jnp.dot(att_rows.T, cot_rows, preferred_element_type=jnp.float32), lax.optimization_barrier(jnp.sum(gain_rows, axis=0)))
        return (tuple((total + round_trip(term) for total, term in zip(carry, terms))), None)
    start = (jnp.zeros((D, HD), jnp.float32), jnp.zeros((D, HD), jnp.float32), jnp.zeros((D, HD), jnp.float32), jnp.zeros((HD, D), jnp.float32), jnp.zeros((D,), jnp.float32))
    totals, _ = lax.scan(accumulate, start, (flat(normed), flat(dquery), flat(dkeys), flat(dvalues), flat(attended), flat(cotangent), flat(gain_terms)))
    grad_query, grad_key, grad_value, grad_out, grad_gain = totals
    return (mixed, grad_tokens, grad_gain, grad_query, grad_key, grad_value, grad_out)
```

```python
import functools

import jax
import jax.numpy as jnp
from jax import lax
from jax.experimental import pallas as pl
from jax.experimental.pallas import tpu as pltpu
from jax.sharding import PartitionSpec as P

MESH = pl.DeviceIdType.MESH
VMEM_LIMIT = 60 * 1024 * 1024


def coords():
    dp, tm = lax.axis_index("dp"), lax.axis_index("tm")
    return lax.div(dp, 2), lax.rem(dp, 2), lax.div(tm, 4), lax.rem(tm, 4)


def device(y, c, z, x):
    return {"dp": y * 2 + c, "tm": z * 4 + x}


def up(p, d):
    return lax.rem(p + d, 4)


def rcopy(src, dst, sems, i, where):
    return pltpu.make_async_remote_copy(
        src_ref=src,
        dst_ref=dst,
        send_sem=sems[0].at[i],
        recv_sem=sems[1].at[i],
        device_id=where,
        device_id_type=MESH,
    )


OFFSETS = [
    (0, 1), (0, 3), (1, 0), (3, 0), (1, 1), (3, 3), (1, 3), (3, 1),
    (2, 2), (0, 2), (2, 0), (2, 1), (2, 3), (1, 2), (3, 2),
]


def greet(y, c, z, x, tm_peers=True):
    barrier = pltpu.get_barrier_semaphore()
    peers = [device(y, 1 - c, z, x)] + [device(up(y, d), c, z, x) for d in (1, 2, 3)]
    peers += [device(y, c, up(z, dz), up(x, dx)) for dz, dx in OFFSETS]
    for peer in peers:
        pl.semaphore_signal(barrier, inc=1, device_id=peer, device_id_type=MESH)
    pl.semaphore_wait(barrier, len(peers))


class Ring:
    def __init__(self, block, half, place, p, sems, first):
        self.block, self.half, self.place, self.p = block, half, place, p
        self.sems, self.first = sems, first

    def start(self):
        p, b = self.p, self.block(self.p)
        self.right = rcopy(b, b, self.sems, self.first, self.place(up(p, 1)))
        self.left = rcopy(b, b, self.sems, self.first + 1, self.place(up(p, 3)))
        self.right.start()
        self.left.start()

    def relay(self):
        p = self.p
        self.right.wait_recv()
        h = self.half(up(p, 3), 0)
        self.on_right = rcopy(h, h, self.sems, self.first + 2, self.place(up(p, 1)))
        self.on_right.start()
        self.left.wait_recv()
        h = self.half(up(p, 1), 1)
        self.on_left = rcopy(h, h, self.sems, self.first + 3, self.place(up(p, 3)))
        self.on_left.start()

    def arrive(self):
        self.on_right.wait_recv()
        self.on_left.wait_recv()

    def finish(self):
        for copy in (self.right, self.left, self.on_right, self.on_left):
            copy.wait_send()


def gather_kernel(tok, cot, wqkv, wo, t_out, c_out, p_out, q_out, ss, sr, a2s, a2r, fs, fr, loc):
    y, c, z, x = coords()
    tm = z * 4 + x
    sib = device(y, 1 - c, z, x)
    greet(y, c, z, x)
    sems, a2, fw = (ss, sr), (a2s, a2r), (fs, fr)
    own = []
    for i, (src, dst) in enumerate(
        [(wqkv.at[c], p_out.at[:, y, c, z, x]), (wo, q_out.at[y, z, x]), (tok.at[tm], t_out.at[c, tm]), (cot.at[tm], c_out.at[c, tm])]
    ):
        copy = pltpu.make_async_copy(src, dst, loc.at[i])
        copy.start()
        own.append(copy)
    s0 = rcopy(wqkv.at[1 - c], p_out.at[:, y, c, z, x], sems, 0, sib)
    s0.start()
    tail = [s0]
    at_x = lambda v: device(y, c, z, v)
    at_y = lambda v: device(v, c, z, x)
    at_z = lambda v: device(y, c, v, x)
    n = 1
    px, pz, py = [], [], []
    for w in range(3):
        px.append(Ring(lambda v, w=w: p_out.at[w, y, :, z, v], lambda v, k, w=w: p_out.at[w, y, k, z, v], at_x, x, sems, n))
        pz.append(Ring(lambda v, w=w: p_out.at[w, y, :, v], lambda v, k, w=w: p_out.at[w, y, k, v], at_z, z, sems, n + 4))
        py.append(Ring(lambda v, w=w: p_out.at[w, v], lambda v, k, w=w: p_out.at[w, v, k], at_y, y, sems, n + 8))
        n += 12
    qy = Ring(lambda v: q_out.at[v, z, x], lambda v, k: q_out.at[v, z, x, :, pl.ds(1024 * k, 1024)], at_y, y, sems, n)
    qx = Ring(lambda v: q_out.at[:, z, v], lambda v, k: q_out.at[pl.ds(2 * k, 2), z, v], at_x, x, sems, n + 4)
    qz = Ring(lambda v: q_out.at[:, v], lambda v, k: q_out.at[pl.ds(2 * k, 2), v], at_z, z, sems, n + 8)

    own[1].wait()
    qy.start()
    own[0].wait()
    s0.wait_recv()
    for r in px:
        r.start()
    sends = []
    for i, (dz, dx) in enumerate(OFFSETS):
        zz, xx = up(z, dz), up(x, dx)
        for j, (src, dst) in enumerate([(tok, t_out), (cot, c_out)]):
            copy = rcopy(src.at[zz * 4 + xx], dst.at[c, tm], a2, 2 * i + j, device(y, c, zz, xx))
            sends.append(copy)
    for r in px:
        r.relay()
    qy.relay()
    for w in range(3):
        px[w].arrive()
        pz[w].start()
    qy.arrive()
    qx.start()
    for w in range(3):
        pz[w].relay()
    qx.relay()
    for w in range(3):
        pz[w].arrive()
        py[w].start()
    qx.arrive()
    qz.start()
    for copy in sends:
        copy.start()
    own[2].wait()
    own[3].wait()
    onward = []
    def pass_on(i, place):
        for j, buf in enumerate((t_out, c_out)):
            copy = rcopy(buf.at[c, place], buf.at[c, place], fw, 2 * i + j, sib)
            copy.start()
            onward.append(copy)
    pass_on(15, tm)
    def fwd(lo, hi):
        for i in range(lo, hi):
            dz, dx = OFFSETS[i]
            sends[2 * i].wait_recv()
            sends[2 * i + 1].wait_recv()
            pass_on(i, up(z, 4 - dz) * 4 + up(x, 4 - dx))
    fwd(0, 5)
    py[0].relay()
    fwd(5, 8)
    py[1].relay()
    qz.relay()
    fwd(8, 12)
    py[2].relay()
    fwd(12, 15)
    for w in range(3):
        py[w].arrive()
    qz.arrive()
    for copy in onward:
        copy.wait_recv()
    for copy in onward + sends + tail:
        copy.wait_send()
    for r in px + pz + py + [qy, qx, qz]:
        r.finish()

def gather_call(tok, cot, wqkv, wo):
    any_ = pl.BlockSpec(memory_space=pl.ANY)
    bf = jnp.bfloat16
    return pl.pallas_call(
        gather_kernel,
        out_shape=(
            jax.ShapeDtypeStruct((2, 16, 24, 2048), bf),
            jax.ShapeDtypeStruct((2, 16, 24, 2048), bf),
            jax.ShapeDtypeStruct((3, 4, 2, 4, 4, 16, 512), bf),
            jax.ShapeDtypeStruct((4, 4, 4, 8, 2048), bf),
        ),
        in_specs=[any_] * 4,
        out_specs=(any_,) * 4,
        scratch_shapes=[
            pltpu.SemaphoreType.DMA((49,)),
            pltpu.SemaphoreType.DMA((49,)),
            pltpu.SemaphoreType.DMA((30,)),
            pltpu.SemaphoreType.DMA((30,)),
            pltpu.SemaphoreType.DMA((32,)),
            pltpu.SemaphoreType.DMA((32,)),
            pltpu.SemaphoreType.DMA((4,)),
        ],
        compiler_params=pltpu.CompilerParams(collective_id=0, has_side_effects=True, vmem_limit_bytes=VMEM_LIMIT),
        name="gather",
    )(tok, cot, wqkv, wo)


def split_weights(w):
    return w.reshape(16, 4, 2, 128).transpose(2, 0, 1, 3).reshape(2, 16, 512)


def nt(a, b):
    return lax.dot_general(a, b, (((1,), (1,)), ((), ())), preferred_element_type=jnp.float32)


def tn(a, b):
    return lax.dot_general(a, b, (((0,), (0,)), ((), ())), preferred_element_type=jnp.float32)


def nn(a, b):
    return jnp.dot(a, b, preferred_element_type=jnp.float32)


FACTOR = 128 ** (-0.5)
BF = jnp.bfloat16
F32 = jnp.float32


def compute_kernel(t, c, w, wo, gain, mp, dp, gp, gq, gg, normed, scaled, proj, back, mask):
    rows_i = lax.broadcasted_iota(jnp.int32, (384, 384), 0)
    cols_i = lax.broadcasted_iota(jnp.int32, (384, 384), 1)
    same = lax.rem(rows_i + 384 - cols_i, 24) == 0
    mask[...] = jnp.where(same & (cols_i <= rows_i), 0.0, -1e30)

    @pl.loop(0, 12)
    def _(i):
        rows = pl.ds(pl.multiple_of(i * 64, 64), 64)
        x = t[rows, :].astype(F32)
        centered = x - jnp.mean(x, axis=-1, keepdims=True)
        inverse = lax.rsqrt(jnp.mean(centered * centered, axis=-1, keepdims=True) + 1e-05)
        s = centered * inverse
        scaled[rows, :] = s
        normed[rows, :] = (s * gain[...]).astype(BF)

    @pl.loop(0, 3)
    def _(i):
        rows = pl.ds(pl.multiple_of(i * 256, 256), 256)
        for k in range(3):
            proj[k, rows, :] = nn(normed[rows, :], w[k]).astype(BF)
        proj[3, rows, :] = nt(c[rows, :], wo[...]).astype(BF)

    @pl.loop(0, 8)
    def _(i):
        rows = pl.ds(pl.multiple_of(lax.div(i, 4) * 384, 128), 384)
        cols = pl.ds(pl.multiple_of(lax.rem(i, 4) * 128, 128), 128)
        q, k, v, u = (proj[j, rows, cols] for j in range(4))
        s = nt(q, k) * FACTOR + mask[...]
        e = jnp.exp(s - jnp.max(s, axis=-1, keepdims=True))
        p = e / jnp.sum(e, axis=-1, keepdims=True)
        p_b = p.astype(BF)
        back[3, rows, cols] = nn(p_b, v).astype(BF)
        d = nt(u, v)
        ds = (p * (d - jnp.sum(p * d, axis=-1, keepdims=True))).astype(BF)
        back[0, rows, cols] = (nn(ds, k) * FACTOR).astype(BF)
        back[1, rows, cols] = (tn(ds, q) * FACTOR).astype(BF)
        back[2, rows, cols] = tn(p_b, u).astype(BF)

    gg[...] = jnp.zeros_like(gg)

    @pl.loop(0, 3)
    def _(i):
        rows = pl.ds(pl.multiple_of(i * 256, 256), 256)
        mp[rows, :] = nn(back[3, rows, :], wo[...]).astype(BF)
        for h in range(2):
            half = pl.ds(h * 1024, 1024)
            dn = nt(back[0, rows, :], w[0, half, :])
            dn += nt(back[1, rows, :], w[1, half, :])
            dn += nt(back[2, rows, :], w[2, half, :])
            dp[rows, half] = dn.astype(BF)
            gg[:, half] += jnp.sum(dn * scaled[rows, half], axis=0, keepdims=True)

    @pl.loop(0, 8)
    def _(i):
        cols = pl.ds(pl.multiple_of(i * 256, 256), 256)
        left = normed[:, cols]
        for k in range(3):
            gp[k, cols, :] = tn(left, back[k]).astype(BF)

    @pl.loop(0, 2)
    def _(i):
        cols = pl.ds(pl.multiple_of(i * 256, 256), 256)
        gq[cols, :] = tn(back[3, :, cols], c[...]).astype(BF)


def compute_call(t, c, w, wo, gain):
    vm = pl.BlockSpec(memory_space=pltpu.VMEM)
    sds = jax.ShapeDtypeStruct
    return pl.pallas_call(
        compute_kernel,
        out_shape=(
            sds((768, 2048), BF),
            sds((768, 2048), BF),
            sds((3, 2048, 512), BF),
            sds((512, 2048), BF),
            sds((1, 2048), F32),
        ),
        in_specs=[vm] * 5,
        out_specs=(vm,) * 5,
        scratch_shapes=[
            pltpu.VMEM((768, 2048), BF),
            pltpu.VMEM((768, 2048), F32),
            pltpu.VMEM((4, 768, 512), BF),
            pltpu.VMEM((4, 768, 512), BF),
            pltpu.VMEM((384, 384), F32),
        ],
        compiler_params=pltpu.CompilerParams(vmem_limit_bytes=VMEM_LIMIT),
        name="attention",
    )(t, c, w, wo, gain)


class RingSum:
    def __init__(self, part, place, p, sems, first, via, land, total, units):
        self.part, self.place, self.p, self.sems, self.first = part, place, p, sems, first
        self.via, self.land, self.total, self.units = via, land, total, units

    def copy(self, i, src, dst, step):
        c = rcopy(src, dst, self.sems, self.first + i, self.place(up(self.p, step)))
        c.start()
        return c

    def start(self):
        p = self.p
        self.a = self.copy(0, self.part(up(p, 2), 0), self.via.at[0], 1)
        self.b = self.copy(1, self.part(up(p, 2), 1), self.via.at[1], 3)
        self.d = self.copy(2, self.part(up(p, 1), 1), self.land.at[0, 1], 1)
        self.e = self.copy(3, self.part(up(p, 3), 0), self.land.at[1, 0], 3)

    def add(self, out, terms):
        lead = out.shape[0]

        @pl.loop(0, lead)
        def _(i):
            value = terms[0][i].astype(F32)
            for term in terms[1:]:
                value = value + term[i].astype(F32)
            out[i] = value.astype(out.dtype)

    def relay(self):
        p = self.p
        self.a.wait_recv()
        self.add(self.via.at[2], [self.via.at[0], self.part(up(p, 1), 0)])
        self.f = self.copy(4, self.via.at[2], self.land.at[0, 0], 1)
        self.b.wait_recv()
        self.add(self.via.at[3], [self.via.at[1], self.part(up(p, 3), 1)])
        self.g = self.copy(5, self.via.at[3], self.land.at[1, 1], 3)

    def finish(self):
        for c in (self.d, self.e, self.f, self.g):
            c.wait_recv()
        for h in range(2):
            self.add(self.total(h), [self.part(self.p, h), self.land.at[0, h], self.land.at[1, h]])

    def drain(self):
        for c in (self.a, self.b, self.d, self.e, self.f, self.g):
            c.wait_send()


def scatter_kernel(t, c_in, mp, dp, gp, gq, gg, gain, mixed, grad, gw, go, gsum,
                   tv, cv, mr, dr, om, og,
                   pvia_y, pland_y, p1, pvia_z, pland_z, p2, pvia_x, pland_x, p3, p3r,
                   qvia_z, qland_z, q1, qvia_x, qland_x, q2, qvia_y, qland_y, q3,
                   gland, gacc, ss, sr, a2s, a2r, gs, gr, ms, mr_sem, loc):
    y, c, z, x = coords()
    tm = z * 4 + x
    sib = device(y, 1 - c, z, x)
    own = []
    for i, (src, dst) in enumerate([(t.at[c], tv), (c_in.at[c], cv)]):
        copy = pltpu.make_async_copy(src, dst, loc.at[i])
        copy.start()
        own.append(copy)
    greet(y, c, z, x)
    sems, a2, gsem, msem = (ss, sr), (a2s, a2r), (gs, gr), (ms, mr_sem)
    at_x = lambda v: device(y, c, z, v)
    at_y = lambda v: device(v, c, z, x)
    at_z = lambda v: device(y, c, v, x)
    swap = []
    for i, (src, dst) in enumerate([(mp, mr), (dp, dr)]):
        for h in range(2):
            rows = pl.ds(8 * h, 8)
            copy = rcopy(src.at[1 - c, rows], dst.at[rows], msem, 2 * i + h, sib)
            copy.start()
            swap.append(copy)
    py, pz, px = [], [], []
    n = 0
    for w in range(3):
        py.append(RingSum(lambda v, h, w=w: gp.at[w, v, h], at_y, y, sems, n, pvia_y.at[w], pland_y.at[w], lambda h, w=w: p1.at[w, h], 4))
        pz.append(RingSum(lambda v, h, w=w: p1.at[w, h, v], at_z, z, sems, n + 6, pvia_z.at[w], pland_z.at[w], lambda h, w=w: p2.at[w, h], 4))
        px.append(RingSum(lambda v, h, w=w: p2.at[w, h, pl.ds(v, 1)], at_x, x, sems, n + 12, pvia_x.at[w], pland_x.at[w], lambda h, w=w: p3.at[w, pl.ds(h, 1)], 1))
        n += 18
    qz = RingSum(lambda v, h: gq.at[pl.ds(2 * h, 2), v], at_z, z, sems, n, qvia_z, qland_z, lambda h: q1.at[pl.ds(2 * h, 2)], 2)
    qx = RingSum(lambda v, h: q1.at[pl.ds(2 * h, 2), v], at_x, x, sems, n + 6, qvia_x, qland_x, lambda h: q2.at[pl.ds(2 * h, 2)], 2)
    qy = RingSum(lambda v, h: q2.at[pl.ds(v, 1), :, pl.ds(1024 * h, 1024)], at_y, y, sems, n + 12, qvia_y, qland_y,
                 lambda h: q3.at[:, :, pl.ds(1024 * h, 1024)], 1)

    def gain_start(k, src):
        place, p = [(at_y, y), (at_z, z), (at_x, x)][k]
        out = []
        for d in (1, 2, 3):
            copy = rcopy(src, gland.at[3 * k + d - 1], gsem, 3 * k + d - 1, place(up(p, d)))
            copy.start()
            out.append(copy)
        return out

    def gain_finish(k, src, copies):
        for copy in copies:
            copy.wait_recv()
        gacc[k] = src[...] + gland[3 * k] + gland[3 * k + 1] + gland[3 * k + 2]

    g0 = gain_start(0, gg)
    for r in py:
        r.start()
    qz.start()
    own[0].wait()
    own[1].wait()
    sends = []

    def finalize(i, f):
        tok = tv[f].astype(F32)
        om[f] = (tok + (mp[c, f].astype(F32) + mr[f].astype(F32))).astype(BF)
        centered = tok - jnp.mean(tok, axis=-1, keepdims=True)
        inverse = lax.rsqrt(jnp.mean(centered * centered, axis=-1, keepdims=True) + 1e-05)
        s = centered * inverse
        ds = (dp[c, f].astype(F32) + dr[f].astype(F32)) * gain[...]
        first = jnp.mean(ds, axis=-1, keepdims=True)
        second = jnp.mean(ds * s, axis=-1, keepdims=True)
        og[f] = (inverse * (ds - first - s * second) + cv[f].astype(F32)).astype(BF)

    for copy in swap:
        copy.wait_recv()
    for i, (dz, dx) in enumerate(OFFSETS):
        zz, xx = up(z, dz), up(x, dx)
        f = zz * 4 + xx
        finalize(i, f)
        for j, (src, dst) in enumerate([(om, mixed), (og, grad)]):
            copy = rcopy(src.at[f], dst.at[tm], a2, 2 * i + j, device(y, c, zz, xx))
            copy.start()
            sends.append(copy)
    finalize(15, tm)
    mine = []
    for j, (src, dst) in enumerate([(om, mixed), (og, grad)]):
        copy = pltpu.make_async_copy(src.at[tm], dst.at[tm], loc.at[2 + j])
        copy.start()
        mine.append(copy)
    gain_finish(0, gg, g0)
    g1 = gain_start(1, gacc.at[0])
    py[0].relay()
    py[1].relay()
    qz.relay()
    py[2].relay()
    py[0].finish()
    pz[0].start()
    gain_finish(1, gacc.at[0], g1)
    g2 = gain_start(2, gacc.at[1])
    py[1].finish()
    pz[1].start()
    qz.finish()
    qx.start()
    pz[0].relay()
    py[2].finish()
    pz[2].start()
    qx.relay()
    pz[1].relay()
    pz[0].finish()
    px[0].start()
    pz[2].relay()
    qx.finish()
    qy.start()
    pz[1].finish()
    px[1].start()
    px[0].relay()
    gain_finish(2, gacc.at[1], g2)
    g3 = rcopy(gacc.at[2], gland.at[9], gsem, 9, sib)
    g3.start()
    pz[2].finish()
    px[2].start()
    qy.relay()
    px[1].relay()
    px[0].finish()
    px[2].relay()
    px[1].finish()
    qy.finish()
    px[2].finish()
    last = []
    for w in range(3):
        copy = rcopy(p3.at[w, 1 - c], p3r.at[w], msem, 4 + w, sib)
        copy.start()
        last.append(copy)
    go[...] = q3[0]
    g3.wait_recv()
    gsum[...] = gacc[2] + gland[9]
    for w in range(3):
        last[w].wait_recv()
        for j in range(4):
            cols = pl.ds(128 * j, 128)
            gw[w, :, pl.ds(pl.multiple_of((2 * j + c) * 128, 128), 128)] = p3[w, c, :, cols]
            gw[w, :, pl.ds(pl.multiple_of((2 * j + 1 - c) * 128, 128), 128)] = p3r[w, :, cols]
    for copy in mine:
        copy.wait()
    for copy in sends:
        copy.wait_recv()
    for copy in sends + swap + g0 + g1 + g2 + [g3] + last:
        copy.wait_send()
    for r in py + pz + px + [qz, qx, qy]:
        r.drain()


def scatter_call(t, c, mp, dp, gp, gq, gg, gain):
    vm = pl.BlockSpec(memory_space=pltpu.VMEM)
    any_ = pl.BlockSpec(memory_space=pl.ANY)
    sds = jax.ShapeDtypeStruct
    V = pltpu.VMEM
    sem = pltpu.SemaphoreType.DMA
    block = (16, 24, 2048)

    def ring(lead, unit):
        return [V(lead + (4,) + unit, BF), V(lead + (2, 2) + unit, BF)]

    return pl.pallas_call(
        scatter_kernel,
        out_shape=(
            sds(block, BF),
            sds(block, BF),
            sds((3, 16, 1024), F32),
            sds((8, 2048), F32),
            sds((16, 128), F32),
        ),
        in_specs=[any_, any_] + [vm] * 6,
        out_specs=(any_, any_, vm, vm, vm),
        scratch_shapes=[V(block, BF)] * 6
        + ring((3,), (4, 4, 16, 512))
        + [V((3, 2, 4, 4, 16, 512), BF)]
        + ring((3,), (4, 16, 512))
        + [V((3, 2, 4, 16, 512), BF)]
        + ring((3,), (1, 16, 512))
        + [V((3, 2, 16, 512), F32), V((3, 16, 512), F32)]
        + ring((), (2, 4, 8, 2048))
        + [V((4, 4, 8, 2048), BF)]
        + ring((), (2, 8, 2048))
        + [V((4, 8, 2048), BF)]
        + ring((), (1, 8, 1024))
        + [V((1, 8, 2048), F32)]
        + [V((10, 16, 128), F32), V((3, 16, 128), F32)]
        + [sem((72,)), sem((72,)), sem((30,)), sem((30,)), sem((10,)), sem((10,)), sem((7,)), sem((7,)), sem((4,))],
        compiler_params=pltpu.CompilerParams(collective_id=1, has_side_effects=True, vmem_limit_bytes=VMEM_LIMIT),
        name="scatter",
    )(t, c, mp, dp, gp, gq, gg, gain)


def on_device(tokens, cotangent, norm_gain, w_query, w_key, w_value, w_out):
    tok = tokens.reshape(16, 24, 2048)
    cot = cotangent.reshape(16, 24, 2048)
    wqkv = jnp.stack([split_weights(w) for w in (w_query, w_key, w_value)], axis=1)
    t, c, wp, wq = gather_call(tok, cot, wqkv, w_out)
    gain = norm_gain.astype(F32).reshape(1, 2048)
    mp, dp, gp, gq, gg = compute_call(
        t.reshape(768, 2048), c.reshape(768, 2048), wp.reshape(3, 2048, 512), wq.reshape(512, 2048), gain
    )
    mixed, grad, gw, go, gsum = scatter_call(
        t,
        c,
        mp.reshape(2, 16, 24, 2048),
        dp.reshape(2, 16, 24, 2048),
        gp.reshape(3, 4, 2, 4, 4, 16, 512),
        gq.reshape(4, 4, 4, 8, 2048),
        gg.reshape(16, 128),
        gain,
    )
    index = lax.axis_index("dp") * 16 + lax.axis_index("tm")
    grad_gain = lax.dynamic_index_in_dim(gsum.reshape(128, 16), index, 0, keepdims=False)
    shape = (1, 1, 384, 2048)
    return mixed.reshape(shape), grad.reshape(shape), grad_gain, gw[0], gw[1], gw[2], go


def solution(mesh):
    rows = P("dp", "tm", None, None)
    weight = P(("dp", "tm"), None)
    return jax.shard_map(
        on_device,
        mesh=mesh,
        in_specs=(rows, rows, P()) + (weight,) * 4,
        out_specs=(rows, rows, P(("dp", "tm"))) + (weight,) * 4,
        check_vma=False,
    )
```

```python
import functools

import jax
import jax.numpy as jnp
from jax import lax
from jax.experimental import pallas as pl
from jax.experimental.pallas import tpu as pltpu
from jax.sharding import PartitionSpec as P

MESH = pl.DeviceIdType.MESH
VMEM_LIMIT = 62 * 1024 * 1024


def coords():
    dp, tm = lax.axis_index("dp"), lax.axis_index("tm")
    return lax.div(dp, 2), lax.rem(dp, 2), lax.div(tm, 4), lax.rem(tm, 4)


def device(y, c, z, x):
    return {"dp": y * 2 + c, "tm": z * 4 + x}


def up(p, d):
    return lax.rem(p + d, 4)


def rcopy(src, dst, sems, i, where):
    return pltpu.make_async_remote_copy(
        src_ref=src,
        dst_ref=dst,
        send_sem=sems[0].at[i],
        recv_sem=sems[1].at[i],
        device_id=where,
        device_id_type=MESH,
    )


OFFSETS = [
    (0, 1), (0, 3), (1, 0), (3, 0), (1, 1), (3, 3), (1, 3), (3, 1),
    (2, 2), (0, 2), (2, 0), (2, 1), (2, 3), (1, 2), (3, 2),
]


def greet(y, c, z, x, tm_peers=True):
    barrier = pltpu.get_barrier_semaphore()
    peers = [device(y, 1 - c, z, x)] + [device(up(y, d), c, z, x) for d in (1, 2, 3)]
    peers += [device(y, c, up(z, dz), up(x, dx)) for dz, dx in OFFSETS]
    for peer in peers:
        pl.semaphore_signal(barrier, inc=1, device_id=peer, device_id_type=MESH)
    pl.semaphore_wait(barrier, len(peers))


class Ring:
    def __init__(self, block, half, place, p, sems, first):
        self.block, self.half, self.place, self.p = block, half, place, p
        self.sems, self.first = sems, first

    def start(self):
        p, b = self.p, self.block(self.p)
        self.right = rcopy(b, b, self.sems, self.first, self.place(up(p, 1)))
        self.left = rcopy(b, b, self.sems, self.first + 1, self.place(up(p, 3)))
        self.right.start()
        self.left.start()

    def relay(self):
        p = self.p
        self.right.wait_recv()
        h = self.half(up(p, 3), 0)
        self.on_right = rcopy(h, h, self.sems, self.first + 2, self.place(up(p, 1)))
        self.on_right.start()
        self.left.wait_recv()
        h = self.half(up(p, 1), 1)
        self.on_left = rcopy(h, h, self.sems, self.first + 3, self.place(up(p, 3)))
        self.on_left.start()

    def arrive(self):
        self.on_right.wait_recv()
        self.on_left.wait_recv()

    def finish(self):
        for copy in (self.right, self.left, self.on_right, self.on_left):
            copy.wait_send()


def nt(a, b):
    return lax.dot_general(a, b, (((1,), (1,)), ((), ())), preferred_element_type=jnp.float32)


def tn(a, b):
    return lax.dot_general(a, b, (((0,), (0,)), ((), ())), preferred_element_type=jnp.float32)


def nn(a, b):
    return jnp.dot(a, b, preferred_element_type=jnp.float32)


FACTOR = 128 ** (-0.5)
BF = jnp.bfloat16
F32 = jnp.float32


class RingSum:
    def __init__(self, part, place, p, sems, first, via, land, total):
        self.part, self.place, self.p, self.sems, self.first = part, place, p, sems, first
        self.via, self.land, self.total = via, land, total

    def copy(self, i, src, dst, step):
        c = rcopy(src, dst, self.sems, self.first + i, self.place(up(self.p, step)))
        c.start()
        return c

    def start(self):
        p = self.p
        self.a = self.copy(0, self.part(up(p, 2), 0), self.via.at[0], 1)
        self.b = self.copy(1, self.part(up(p, 2), 1), self.via.at[1], 3)
        self.d = self.copy(2, self.part(up(p, 1), 1), self.land.at[0, 1], 1)
        self.e = self.copy(3, self.part(up(p, 3), 0), self.land.at[1, 0], 3)

    def add(self, out, terms):
        lead = out.shape[0]

        @pl.loop(0, lead)
        def _(i):
            value = terms[0][i].astype(F32)
            for term in terms[1:]:
                value = value + term[i].astype(F32)
            out[i] = value.astype(out.dtype)

    def relay(self):
        p = self.p
        self.a.wait_recv()
        self.add(self.via.at[2], [self.via.at[0], self.part(up(p, 1), 0)])
        self.f = self.copy(4, self.via.at[2], self.land.at[0, 0], 1)
        self.b.wait_recv()
        self.add(self.via.at[3], [self.via.at[1], self.part(up(p, 3), 1)])
        self.g = self.copy(5, self.via.at[3], self.land.at[1, 1], 3)

    def finish(self):
        for c in (self.d, self.e, self.f, self.g):
            c.wait_recv()
        for h in range(2):
            self.add(self.total(h), [self.part(self.p, h), self.land.at[0, h], self.land.at[1, h]])

    def drain(self):
        for c in (self.a, self.b, self.d, self.e, self.f, self.g):
            c.wait_send()


def wait_bytes(ref, sem):
    pltpu.make_async_copy(ref, ref, sem).wait()


def block_kernel(tok, cot, wq, wk, wv, w_out, gain, mixed, grad, g_q, g_k, g_v, g_o, gsum,
                 t, ct, w, wo, wom, normed, cotm, scaled, proj, back, mask, mp, dp, mr, dr, om, og,
                 via1, land1, sum1, via2, land2, sum2, via3, land3, p3, p3r,
                 qvia1, qland1, q1, qvia2, qland2, q2, qvia3, qland3, q3,
                 gg, gland, gacc,
                 ag_s, ag_r, w_s, w_r, w_l, in_s, in_r, fw_s, fw_r, sw_s, sw_r, bk_s, bk_r, rs_s, rs_r, gn_s, gn_r, loc):
    y, c, z, x = coords()
    tm = z * 4 + x
    sib = device(y, 1 - c, z, x)
    at_x = lambda v: device(y, c, z, v)
    at_y = lambda v: device(v, c, z, x)
    at_z = lambda v: device(y, c, v, x)

    stage = []
    for j, (src, dst) in enumerate([(tok, om), (cot, og)]):
        for g in range(3):
            copy = pltpu.make_async_copy(src.at[:, g], dst.at[g], loc.at[3 * j + g])
            copy.start()
            stage.append(copy)
    own_o = pltpu.make_async_copy(w_out, wo.at[y, z, x], loc.at[6])
    own_o.start()
    own_w = []
    for i, src in enumerate((wq, wk, wv)):
        for j in range(4):
            cols = pl.ds(pl.multiple_of((2 * j + c) * 128, 128), 128)
            copy = pltpu.make_async_copy(src.at[:, cols], w.at[i, y, c, z, x, :, pl.ds(128 * j, 128)], w_l.at[4 * i + j])
            copy.start()
            own_w.append(copy)
    greet(y, c, z, x)

    swap_w = []
    for i, src in enumerate((wq, wk, wv)):
        for j in range(4):
            cols = pl.ds(pl.multiple_of((2 * j + 1 - c) * 128, 128), 128)
            copy = rcopy(src.at[:, cols], w.at[i, y, c, z, x, :, pl.ds(128 * j, 128)], (w_s, w_r), 4 * i + j, sib)
            copy.start()
            swap_w.append(copy)

    ag = (ag_s, ag_r)

    def yx(i):
        a = Ring(lambda v: w.at[i, y, :, z, v], lambda v, k: w.at[i, y, k, z, v], at_x, x, ag, 12 * i)
        b = Ring(lambda v: w.at[i, y, :, v], lambda v, k: w.at[i, y, k, v], at_z, z, ag, 12 * i + 4)
        d = Ring(lambda v: w.at[i, v], lambda v, k: w.at[i, v, k], at_y, y, ag, 12 * i + 8)
        return a, b, d

    qa, qb, qc = yx(0)
    ka, kb, kc = yx(1)
    va = Ring(lambda v: w.at[2, v, :, z, x], lambda v, k: w.at[2, v, k, z, x], at_y, y, ag, 24)
    vb = Ring(lambda v: w.at[2, :, :, v, x], lambda v, k: w.at[2, :, k, v, x], at_z, z, ag, 28)
    vc = Ring(lambda v: w.at[2, :, :, :, v], lambda v, k: w.at[2, :, k, :, v], at_x, x, ag, 32)
    oa = Ring(lambda v: wo.at[v, z, x], lambda v, k: wo.at[v, z, x, :, pl.ds(1024 * k, 1024)], at_y, y, ag, 36)
    ob = Ring(lambda v: wo.at[:, z, v], lambda v, k: wo.at[pl.ds(2 * k, 2), z, v], at_x, x, ag, 40)
    oc = Ring(lambda v: wo.at[:, v], lambda v, k: wo.at[pl.ds(2 * k, 2), v], at_z, z, ag, 44)
    rings = (qa, qb, qc, ka, kb, kc, va, vb, vc, oa, ob, oc)

    own_o.wait()
    oa.start()
    for copy in own_w:
        copy.wait()
    for copy in swap_w:
        copy.wait_recv()
    for r in (qa, va, ka):
        r.start()

    def spread(g):
        for j, (src, staged, dst) in enumerate([(tok, om, t), (cot, og, ct)]):
            stage[3 * j + g].wait()
            pltpu.make_async_copy(src.at[tm, g], dst.at[c, g, tm], in_r.at[2 * g + j]).start()
        for dz, dx in OFFSETS:
            zz, xx = up(z, dz), up(x, dx)
            for j, (staged, dst) in enumerate([(om, t), (og, ct)]):
                rcopy(staged.at[g, zz * 4 + xx], dst.at[c, g, tm], (in_s, in_r), 2 * g + j, device(y, c, zz, xx)).start()

    passed = {}

    def pass_on(g):
        passed[g] = []
        for j, dst in enumerate((t, ct)):
            wait_bytes(dst.at[c, g], in_r.at[2 * g + j])
            copy = rcopy(dst.at[c, g], dst.at[c, g], (fw_s, fw_r), 2 * g + j, sib)
            copy.start()
            passed[g].append(copy)

    def norm(g):
        for copy in passed[g]:
            copy.wait_recv()

        @pl.loop(0, 8)
        def _(i):
            k, f = lax.div(i, 4), lax.rem(i, 4) * 4
            value = t[k, g, pl.ds(f, 4)].astype(F32).reshape(32, 2048)
            centered = value - jnp.mean(value, axis=-1, keepdims=True)
            inverse = lax.rsqrt(jnp.mean(centered * centered, axis=-1, keepdims=True) + 1e-05)
            s = centered * inverse
            scaled[pl.ds(pl.multiple_of(i * 32, 32), 32), :] = s
            rows = pl.ds(pl.multiple_of(g * 256 + i * 32, 32), 32)
            normed[rows, :] = (s * gain[...]).astype(BF)
            cotm[rows, :] = ct[k, g, pl.ds(f, 4)].astype(F32).reshape(32, 2048).astype(BF)

    def project(g, i):
        rows = pl.ds(g * 256, 256)
        if i < 3:
            proj[i] = nn(normed[rows, :], w[i].reshape(2048, 512)).astype(BF)
        else:
            proj[3] = nt(cotm[rows, :], wom[...]).astype(BF)

    def attention(g):
        @pl.loop(0, 4)
        def _(h):
            cols = pl.ds(pl.multiple_of(h * 128, 128), 128)
            for clip in range(2):
                rows = pl.ds(clip * 128, 128)
                out = pl.ds(g * 256 + clip * 128, 128)
                q, k, v, u = (proj[j, rows, cols] for j in range(4))
                s = nt(q, k) * FACTOR + mask[...]
                e = jnp.exp(s - jnp.max(s, axis=-1, keepdims=True))
                p = e / jnp.sum(e, axis=-1, keepdims=True)
                p_b = p.astype(BF)
                back[3, out, cols] = nn(p_b, v).astype(BF)
                d = nt(u, v)
                ds = (p * (d - jnp.sum(p * d, axis=-1, keepdims=True))).astype(BF)
                back[0, out, cols] = (nn(ds, k) * FACTOR).astype(BF)
                back[1, out, cols] = (tn(ds, q) * FACTOR).astype(BF)
                back[2, out, cols] = tn(p_b, u).astype(BF)

    swapped = {}

    def partials(g):
        rows = pl.ds(g * 256, 256)
        for h in range(2):
            half = pl.ds(h * 1024, 1024)
            mp[g, :, :, :, half] = nn(back[3, rows, :], wom[:, half]).reshape(2, 16, 8, 1024).astype(BF)
            dn = None
            for i in range(3):
                term = nt(back[i, rows, :], w[i, pl.ds(2 * h, 2)].reshape(1024, 512))
                dn = term if dn is None else dn + term
            dp[g, :, :, :, half] = dn.reshape(2, 16, 8, 1024).astype(BF)
            total = jnp.sum(dn * scaled[:, half], axis=0, keepdims=True)
            gg[:, half] = total if g == 0 else gg[:, half] + total
        swapped[g] = []
        for j, (src, dst) in enumerate([(mp, mr), (dp, dr)]):
            copy = rcopy(src.at[g, 1 - c], dst.at[g], (sw_s, sw_r), 2 * g + j, sib)
            copy.start()
            swapped[g].append(copy)

    def finalize(g):
        for j, staged in enumerate((om, og)):
            wait_bytes(staged.at[g, pl.ds(0, 15)], in_s.at[2 * g + j])
        for copy in swapped[g]:
            copy.wait_recv()

        @pl.loop(0, 4)
        def _(i):
            fs = pl.ds(i * 4, 4)
            value = t[c, g, fs].astype(F32)
            om[g, fs] = (value + (mp[g, c, fs].astype(F32) + mr[g, fs].astype(F32))).astype(BF)
            centered = value - jnp.mean(value, axis=-1, keepdims=True)
            inverse = lax.rsqrt(jnp.mean(centered * centered, axis=-1, keepdims=True) + 1e-05)
            s = centered * inverse
            ds = (dp[g, c, fs].astype(F32) + dr[g, fs].astype(F32)) * gain[...].reshape(1, 1, 2048)
            first = jnp.mean(ds, axis=-1, keepdims=True)
            second = jnp.mean(ds * s, axis=-1, keepdims=True)
            og[g, fs] = (inverse * (ds - first - s * second) + ct[c, g, fs].astype(F32)).astype(BF)

        for dz, dx in OFFSETS:
            zz, xx = up(z, dz), up(x, dx)
            for j, (src, dst) in enumerate([(om, mixed), (og, grad)]):
                rcopy(src.at[g, zz * 4 + xx], dst.at[tm, g], (bk_s, bk_r), j, device(y, c, zz, xx)).start()
        for j, (src, dst) in enumerate([(om, mixed), (og, grad)]):
            pltpu.make_async_copy(src.at[g, tm], dst.at[tm, g], bk_r.at[j]).start()

    def w_terms(i):
        @pl.loop(0, 8)
        def _(b):
            cols = pl.ds(pl.multiple_of(b * 256, 256), 256)
            w[i, lax.div(b, 2), lax.rem(b, 2)] = tn(normed[:, cols], back[i]).reshape(4, 4, 16, 512).astype(BF)

    def o_terms():
        @pl.loop(0, 2)
        def _(b):
            cols = pl.ds(pl.multiple_of(b * 256, 256), 256)
            wo[pl.ds(2 * b, 2)] = tn(back[3, :, cols], cotm[...]).reshape(2, 4, 4, 8, 2048).astype(BF)

    rs = (rs_s, rs_r)

    def sums(i):
        if i < 2:
            a = RingSum(lambda v, h: w.at[i, v, h], at_y, y, rs, 18 * i, via1.at[i], land1.at[i], lambda h: sum1.at[i, h])
            b = RingSum(lambda v, h: sum1.at[i, h, v], at_z, z, rs, 18 * i + 6, via2.at[i], land2.at[i], lambda h: sum2.at[i, h])
            d = RingSum(lambda v, h: sum2.at[i, h, pl.ds(v, 1)], at_x, x, rs, 18 * i + 12, via3.at[i], land3.at[i],
                        lambda h: p3.at[i, pl.ds(h, 1)])
        else:
            a = RingSum(lambda v, h: w.at[i, :, h, :, v], at_x, x, rs, 18 * i, via1.at[i], land1.at[i], lambda h: sum1.at[i, h])
            b = RingSum(lambda v, h: sum1.at[i, h, :, v], at_z, z, rs, 18 * i + 6, via2.at[i], land2.at[i], lambda h: sum2.at[i, h])
            d = RingSum(lambda v, h: sum2.at[i, h, pl.ds(v, 1)], at_y, y, rs, 18 * i + 12, via3.at[i], land3.at[i],
                        lambda h: p3.at[i, pl.ds(h, 1)])
        return a, b, d

    qx, qy, qz = sums(0)
    kx, ky, kz = sums(1)
    vx, vy, vz = sums(2)
    ox = RingSum(lambda v, h: wo.at[pl.ds(2 * h, 2), v], at_z, z, rs, 54, qvia1, qland1, lambda h: q1.at[pl.ds(2 * h, 2)])
    oy = RingSum(lambda v, h: q1.at[pl.ds(2 * h, 2), v], at_x, x, rs, 60, qvia2, qland2, lambda h: q2.at[pl.ds(2 * h, 2)])
    oz = RingSum(lambda v, h: q2.at[pl.ds(v, 1), :, pl.ds(1024 * h, 1024)], at_y, y, rs, 66, qvia3, qland3,
                 lambda h: q3.at[:, :, pl.ds(1024 * h, 1024)])
    all_sums = (qx, qy, qz, kx, ky, kz, vx, vy, vz, ox, oy, oz)

    def gain_start(k, src):
        place, p = [(at_y, y), (at_z, z), (at_x, x)][k]
        out = []
        for d in (1, 2, 3):
            copy = rcopy(src, gland.at[3 * k + d - 1], (gn_s, gn_r), 3 * k + d - 1, place(up(p, d)))
            copy.start()
            out.append(copy)
        return out

    def gain_finish(k, src, copies):
        for copy in copies:
            copy.wait_recv()
        gacc[k] = src[...] + gland[3 * k] + gland[3 * k + 1] + gland[3 * k + 2]

    spread(0)
    rows_i = lax.broadcasted_iota(jnp.int32, (128, 128), 0)
    cols_i = lax.broadcasted_iota(jnp.int32, (128, 128), 1)
    same = lax.rem(rows_i + 128 - cols_i, 8) == 0
    mask[...] = jnp.where(same & (cols_i <= rows_i), 0.0, -1e30)
    for r in (qa, oa, va, ka):
        r.relay()
    for a, b in ((qa, qb), (oa, ob), (va, vb), (ka, kb)):
        a.arrive()
        b.start()
    for r in (qb, ob, vb, kb):
        r.relay()
    for a, b in ((qb, qc), (ob, oc), (vb, vc), (kb, kc)):
        a.arrive()
        b.start()
    pass_on(0)
    norm(0)
    qc.relay()
    vc.relay()
    oc.relay()
    spread(1)
    kc.relay()
    spread(2)
    qc.arrive()
    project(0, 0)
    vc.arrive()
    project(0, 2)
    oc.arrive()

    @pl.loop(0, 4)
    def _(j):
        wom[pl.ds(pl.multiple_of(j * 128, 128), 128), :] = wo[j].astype(F32).reshape(128, 2048).astype(BF)

    project(0, 3)
    kc.arrive()
    project(0, 1)
    attention(0)
    pass_on(1)
    partials(0)
    norm(1)
    for i in range(4):
        project(1, i)
    finalize(0)
    attention(1)
    pass_on(2)
    partials(1)
    norm(2)
    for i in range(4):
        project(2, i)
    finalize(1)
    attention(2)
    partials(2)
    for i in range(16):
        gland[9, pl.ds(i, 1), :] = gg[:, pl.ds(128 * i, 128)]
    g0 = gain_start(0, gland.at[9])
    for r in rings:
        r.finish()
    w_terms(1)
    kx.start()
    w_terms(2)
    vx.start()
    finalize(2)
    o_terms()
    ox.start()
    kx.relay()
    w_terms(0)
    qx.start()
    vx.relay()
    ox.relay()
    gain_finish(0, gland.at[9], g0)
    g1 = gain_start(1, gacc.at[0])
    kx.finish()
    ky.start()
    qx.relay()
    vx.finish()
    vy.start()
    ox.finish()
    oy.start()
    ky.relay()
    gain_finish(1, gacc.at[0], g1)
    g2 = gain_start(2, gacc.at[1])
    vy.relay()
    oy.relay()
    ky.finish()
    kz.start()
    qx.finish()
    qy.start()
    vy.finish()
    vz.start()
    oy.finish()
    oz.start()
    kz.relay()
    vz.relay()
    oz.relay()
    qy.relay()
    gain_finish(2, gacc.at[1], g2)
    g3 = rcopy(gacc.at[2], gland.at[10], (gn_s, gn_r), 9, sib)
    g3.start()
    last = {}

    def across(i):
        copy = rcopy(p3.at[i, 1 - c], p3r.at[i], (sw_s, sw_r), 6 + i, sib)
        copy.start()
        last[i] = copy

    def put(i, out):
        last[i].wait_recv()
        for j in range(4):
            cols = pl.ds(128 * j, 128)
            out[:, pl.ds(pl.multiple_of((2 * j + c) * 128, 128), 128)] = p3[i, c, :, cols]
            out[:, pl.ds(pl.multiple_of((2 * j + 1 - c) * 128, 128), 128)] = p3r[i, :, cols]

    kz.finish()
    across(1)
    qy.finish()
    qz.start()
    vz.finish()
    across(2)
    oz.finish()
    g_o[...] = q3[0]
    put(1, g_k)
    qz.relay()
    put(2, g_v)
    g3.wait_recv()
    gsum[...] = gacc[2] + gland[10]
    qz.finish()
    across(0)
    put(0, g_q)
    for j, (src, dst) in enumerate([(om, mixed), (og, grad)]):
        wait_bytes(dst, bk_r.at[j])
        wait_bytes(src.at[:, pl.ds(0, 15)], bk_s.at[j])
    for copies in (swap_w, passed[0], passed[1], passed[2], swapped[0], swapped[1], swapped[2], g0, g1, g2, [g3], list(last.values())):
        for copy in copies:
            copy.wait_send()
    for r in all_sums:
        r.drain()


def block_call(tok, cot, wq, wk, wv, w_out, gain):
    vm = pl.BlockSpec(memory_space=pltpu.VMEM)
    any_ = pl.BlockSpec(memory_space=pl.ANY)
    sds = jax.ShapeDtypeStruct
    V = pltpu.VMEM
    sem = pltpu.SemaphoreType.DMA
    rows = (16, 3, 8, 2048)
    groups = (3, 16, 8, 2048)

    def ring(lead, unit):
        return [V(lead + (4,) + unit, BF), V(lead + (2, 2) + unit, BF)]

    sems = [48, 48, 12, 12, 12, 6, 6, 6, 6, 9, 9, 2, 2, 72, 72, 10, 10, 7]
    return pl.pallas_call(
        block_kernel,
        out_shape=(sds(rows, BF), sds(rows, BF))
        + (sds((16, 1024), F32),) * 3
        + (sds((8, 2048), F32), sds((16, 128), F32)),
        in_specs=[any_] * 6 + [vm],
        out_specs=(any_, any_) + (vm,) * 5,
        scratch_shapes=[V((2, 3, 16, 8, 2048), BF)] * 2
        + [V((3, 4, 2, 4, 4, 16, 512), BF), V((4, 4, 4, 8, 2048), BF), V((512, 2048), BF)]
        + [V((768, 2048), BF)] * 2
        + [V((256, 2048), F32), V((4, 256, 512), BF), V((4, 768, 512), BF), V((128, 128), F32)]
        + [V((3, 2, 16, 8, 2048), BF)] * 2
        + [V(groups, BF)] * 4
        + ring((3,), (4, 4, 16, 512))
        + [V((3, 2, 4, 4, 16, 512), BF)]
        + ring((3,), (4, 16, 512))
        + [V((3, 2, 4, 16, 512), BF)]
        + ring((3,), (1, 16, 512))
        + [V((3, 2, 16, 512), F32), V((3, 16, 512), F32)]
        + ring((), (2, 4, 8, 2048))
        + [V((4, 4, 8, 2048), BF)]
        + ring((), (2, 8, 2048))
        + [V((4, 8, 2048), BF)]
        + ring((), (1, 8, 1024))
        + [V((1, 8, 2048), F32)]
        + [V((1, 2048), F32), V((11, 16, 128), F32), V((3, 16, 128), F32)]
        + [sem((n,)) for n in sems],
        compiler_params=pltpu.CompilerParams(collective_id=0, has_side_effects=True, vmem_limit_bytes=VMEM_LIMIT),
        name="block",
    )(tok, cot, wq, wk, wv, w_out, gain)


def on_device(tokens, cotangent, norm_gain, w_query, w_key, w_value, w_out):
    tok = tokens.reshape(16, 3, 8, 2048)
    cot = cotangent.reshape(16, 3, 8, 2048)
    gain = norm_gain.astype(F32).reshape(1, 2048)
    mixed, grad, g_q, g_k, g_v, g_o, gsum = block_call(tok, cot, w_query, w_key, w_value, w_out, gain)
    index = lax.axis_index("dp") * 16 + lax.axis_index("tm")
    grad_gain = lax.dynamic_index_in_dim(gsum.reshape(128, 16), index, 0, keepdims=False)
    shape = (1, 1, 384, 2048)
    return mixed.reshape(shape), grad.reshape(shape), grad_gain, g_q, g_k, g_v, g_o


def solution(mesh):
    rows = P("dp", "tm", None, None)
    weight = P(("dp", "tm"), None)
    return jax.shard_map(
        on_device,
        mesh=mesh,
        in_specs=(rows, rows, P()) + (weight,) * 4,
        out_specs=(rows, rows, P(("dp", "tm"))) + (weight,) * 4,
        check_vma=False,
    )
```

```python
import functools

import jax
import jax.numpy as jnp
from jax import lax
from jax.experimental import pallas as pl
from jax.experimental.pallas import tpu as pltpu
from jax.sharding import PartitionSpec as P

MESH = pl.DeviceIdType.MESH
CUT = 1024
VMEM_LIMIT = 62 * 1024 * 1024


def coords():
    dp, tm = lax.axis_index("dp"), lax.axis_index("tm")
    return lax.div(dp, 2), lax.rem(dp, 2), lax.div(tm, 4), lax.rem(tm, 4)


def device(y, c, z, x):
    return {"dp": y * 2 + c, "tm": z * 4 + x}


def up(p, d):
    return lax.rem(p + d, 4)


def rcopy(src, dst, sems, i, where):
    return pltpu.make_async_remote_copy(
        src_ref=src,
        dst_ref=dst,
        send_sem=sems[0].at[i],
        recv_sem=sems[1].at[i],
        device_id=where,
        device_id_type=MESH,
    )


OFFSETS = [
    (0, 1), (0, 3), (1, 0), (3, 0), (1, 1), (3, 3), (1, 3), (3, 1),
    (2, 2), (0, 2), (2, 0), (2, 1), (2, 3), (1, 2), (3, 2),
]


def greet(y, c, z, x, tm_peers=True):
    barrier = pltpu.get_barrier_semaphore()
    peers = [device(y, 1 - c, z, x)] + [device(up(y, d), c, z, x) for d in (1, 2, 3)]
    peers += [device(y, c, up(z, dz), up(x, dx)) for dz, dx in OFFSETS]
    for peer in peers:
        pl.semaphore_signal(barrier, inc=1, device_id=peer, device_id_type=MESH)
    pl.semaphore_wait(barrier, len(peers))


class Ring:
    def __init__(self, block, half, place, p, sems, first):
        self.block, self.half, self.place, self.p = block, half, place, p
        self.sems, self.first = sems, first

    def start(self):
        p, b = self.p, self.block(self.p)
        self.right = rcopy(b, b, self.sems, self.first, self.place(up(p, 1)))
        self.left = rcopy(b, b, self.sems, self.first + 1, self.place(up(p, 3)))
        self.right.start()
        self.left.start()

    def relay(self):
        p = self.p
        self.right.wait_recv()
        h = self.half(up(p, 3), 0)
        self.on_right = rcopy(h, h, self.sems, self.first + 2, self.place(up(p, 1)))
        self.on_right.start()
        self.left.wait_recv()
        h = self.half(up(p, 1), 1)
        self.on_left = rcopy(h, h, self.sems, self.first + 3, self.place(up(p, 3)))
        self.on_left.start()

    def arrive(self):
        self.on_right.wait_recv()
        self.on_left.wait_recv()

    def finish(self):
        for copy in (self.right, self.left, self.on_right, self.on_left):
            copy.wait_send()


class Direct:
    def __init__(self, block, place, p, sems, first):
        b = block(p)
        self.copies = [rcopy(b, b, sems, first + d - 1, place(up(p, d))) for d in (1, 2, 3)]

    def start(self):
        for copy in self.copies:
            copy.start()

    def arrive(self):
        for copy in self.copies:
            copy.wait_recv()

    def finish(self):
        for copy in self.copies:
            copy.wait_send()


def nt(a, b):
    return lax.dot_general(a, b, (((1,), (1,)), ((), ())), preferred_element_type=jnp.float32)


def tn(a, b):
    return lax.dot_general(a, b, (((0,), (0,)), ((), ())), preferred_element_type=jnp.float32)


def nn(a, b):
    return jnp.dot(a, b, preferred_element_type=jnp.float32)


FACTOR = 128 ** (-0.5)
BF = jnp.bfloat16
F32 = jnp.float32


def add(out, terms):
    @pl.loop(0, out.shape[0])
    def _(i):
        value = terms[0][i].astype(F32)
        for term in terms[1:]:
            value = value + term[i].astype(F32)
        out[i] = value.astype(out.dtype)


class DirectSum:
    def __init__(self, part, place, p, sems, first, land, total):
        self.own, self.land, self.total = part(p), land, total
        self.copies = [rcopy(part(up(p, d)), land.at[d - 1], sems, first + d - 1, place(up(p, d))) for d in (1, 2, 3)]

    def start(self):
        for copy in self.copies:
            copy.start()

    def finish(self):
        for copy in self.copies:
            copy.wait_recv()
        add(self.total, [self.own] + [self.land.at[d] for d in range(3)])

    def drain(self):
        for copy in self.copies:
            copy.wait_send()


class RingSum:
    def __init__(self, part, place, p, sems, first, via, land, total):
        self.part, self.place, self.p, self.sems, self.first = part, place, p, sems, first
        self.via, self.land, self.total = via, land, total

    def copy(self, i, src, dst, step):
        c = rcopy(src, dst, self.sems, self.first + i, self.place(up(self.p, step)))
        c.start()
        return c

    def start(self):
        p = self.p
        self.a = self.copy(0, self.part(up(p, 2), 0), self.via.at[0], 1)
        self.b = self.copy(1, self.part(up(p, 2), 1), self.via.at[1], 3)
        self.d = self.copy(2, self.part(up(p, 1), 1), self.land.at[0, 1], 1)
        self.e = self.copy(3, self.part(up(p, 3), 0), self.land.at[1, 0], 3)

    def relay(self):
        p = self.p
        self.a.wait_recv()
        add(self.via.at[2], [self.via.at[0], self.part(up(p, 1), 0)])
        self.f = self.copy(4, self.via.at[2], self.land.at[0, 0], 1)
        self.b.wait_recv()
        add(self.via.at[3], [self.via.at[1], self.part(up(p, 3), 1)])
        self.g = self.copy(5, self.via.at[3], self.land.at[1, 1], 3)

    def finish(self):
        for c in (self.d, self.e, self.f, self.g):
            c.wait_recv()
        for h in range(2):
            add(self.total(h), [self.part(self.p, h), self.land.at[0, h], self.land.at[1, h]])

    def drain(self):
        for c in (self.a, self.b, self.d, self.e, self.f, self.g):
            c.wait_send()


def wait_bytes(ref, sem):
    pltpu.make_async_copy(ref, ref, sem).wait()


def block_kernel(tok, cot, wq, wk, wv, w_out, gain, mixed, grad, g_q, g_k, g_v, g_o, gsum,
                 t, ct, w, wo, wom, normed, cotm, scaled, proj, back, mask, mp, dp, mr, dr, om, og,
                 via1, land1, sum1, land2, sum2, land3, p3, p3r,
                 dvia, dland, d1, dland2, d2, dland3, evia, eland, e1, eland2, e2, eland3,
                 fvia, fland, f1, fland2, f2, fland3, q3,
                 gg, gland, gacc,
                 ag_s, ag_r, w_s, w_r, w_l, in_s, in_r, fw_s, fw_r, sw_s, sw_r, bk_s, bk_r, rs_s, rs_r, gn_s, gn_r, loc):
    y, c, z, x = coords()
    tm = z * 4 + x
    sib = device(y, 1 - c, z, x)
    at_x = lambda v: device(y, c, z, v)
    at_y = lambda v: device(v, c, z, x)
    at_z = lambda v: device(y, c, v, x)

    stage = []
    for j, (src, dst) in enumerate([(tok, om), (cot, og)]):
        for g in range(3):
            copy = pltpu.make_async_copy(src.at[:, g], dst.at[g], loc.at[3 * j + g])
            copy.start()
            stage.append(copy)
    own_o = pltpu.make_async_copy(w_out, wo.at[y, z, x], loc.at[6])
    own_o.start()
    own_w = []
    for i, src in enumerate((wq, wk, wv)):
        for j in range(4):
            cols = pl.ds(pl.multiple_of((2 * j + c) * 128, 128), 128)
            copy = pltpu.make_async_copy(src.at[:, cols], w.at[i, y, c, z, x, :, pl.ds(128 * j, 128)], w_l.at[4 * i + j])
            copy.start()
            own_w.append(copy)
    greet(y, c, z, x)

    swap_w = []
    for i, src in enumerate((wq, wk, wv)):
        for j in range(4):
            cols = pl.ds(pl.multiple_of((2 * j + 1 - c) * 128, 128), 128)
            copy = rcopy(src.at[:, cols], w.at[i, y, c, z, x, :, pl.ds(128 * j, 128)], (w_s, w_r), 4 * i + j, sib)
            copy.start()
            swap_w.append(copy)

    ag = (ag_s, ag_r)

    qa = Direct(lambda v: w.at[0, y, :, z, v], at_x, x, ag, 0)
    qb = Direct(lambda v: w.at[0, y, :, v], at_z, z, ag, 3)
    qc = Ring(lambda v: w.at[0, v], lambda v, k: w.at[0, v, k], at_y, y, ag, 6)
    ka = Direct(lambda v: w.at[1, y, :, v, x], at_z, z, ag, 10)
    kb = Direct(lambda v: w.at[1, v, :, :, x], at_y, y, ag, 13)
    kc = Ring(lambda v: w.at[1, :, :, :, v], lambda v, k: w.at[1, :, k, :, v], at_x, x, ag, 16)
    va = Direct(lambda v: w.at[2, v, :, z, x], at_y, y, ag, 20)
    vb = Direct(lambda v: w.at[2, :, :, z, v], at_x, x, ag, 23)
    vc = Ring(lambda v: w.at[2, :, :, v], lambda v, k: w.at[2, :, k, v], at_z, z, ag, 26)
    o0, o1, o2 = (pl.ds(0, CUT), pl.ds(CUT, (2048 - CUT) // 2), pl.ds(CUT + (2048 - CUT) // 2, (2048 - CUT) // 2))
    da = Direct(lambda v: wo.at[y, v, x, :, o0], at_z, z, ag, 30)
    db = Direct(lambda v: wo.at[y, :, v, :, o0], at_x, x, ag, 33)
    dc = Ring(lambda v: wo.at[v, :, :, :, o0], lambda v, k: wo.at[v, pl.ds(2 * k, 2), :, :, o0], at_y, y, ag, 36)
    ea = Direct(lambda v: wo.at[v, z, x, :, o1], at_y, y, ag, 40)
    eb = Direct(lambda v: wo.at[:, v, x, :, o1], at_z, z, ag, 43)
    ec = Ring(lambda v: wo.at[:, :, v, :, o1], lambda v, k: wo.at[pl.ds(2 * k, 2), :, v, :, o1], at_x, x, ag, 46)
    fa = Direct(lambda v: wo.at[y, z, v, :, o2], at_x, x, ag, 50)
    fb = Direct(lambda v: wo.at[v, z, :, :, o2], at_y, y, ag, 53)
    fc = Ring(lambda v: wo.at[:, v, :, :, o2], lambda v, k: wo.at[pl.ds(2 * k, 2), v, :, :, o2], at_z, z, ag, 56)
    firsts, seconds, thirds = (qa, ka, va, da, ea, fa), (qb, kb, vb, db, eb, fb), (qc, kc, vc, dc, ec, fc)
    rings = firsts + seconds + thirds

    def spread(g):
        for j, (src, staged, dst) in enumerate([(tok, om, t), (cot, og, ct)]):
            stage[3 * j + g].wait()
            pltpu.make_async_copy(src.at[tm, g], dst.at[c, g, tm], in_r.at[2 * g + j]).start()
        for dz, dx in OFFSETS:
            zz, xx = up(z, dz), up(x, dx)
            for j, (staged, dst) in enumerate([(om, t), (og, ct)]):
                rcopy(staged.at[g, zz * 4 + xx], dst.at[c, g, tm], (in_s, in_r), 2 * g + j, device(y, c, zz, xx)).start()

    passed = {}

    def pass_on(g):
        passed[g] = []
        for j, dst in enumerate((t, ct)):
            wait_bytes(dst.at[c, g], in_r.at[2 * g + j])
            copy = rcopy(dst.at[c, g], dst.at[c, g], (fw_s, fw_r), 2 * g + j, sib)
            copy.start()
            passed[g].append(copy)

    def norm(g):
        for copy in passed[g]:
            copy.wait_recv()

        @pl.loop(0, 8)
        def _(i):
            k, f = lax.div(i, 4), lax.rem(i, 4) * 4
            value = t[k, g, pl.ds(f, 4)].astype(F32).reshape(32, 2048)
            centered = value - jnp.mean(value, axis=-1, keepdims=True)
            inverse = lax.rsqrt(jnp.mean(centered * centered, axis=-1, keepdims=True) + 1e-05)
            s = centered * inverse
            scaled[pl.ds(pl.multiple_of(i * 32, 32), 32), :] = s
            rows = pl.ds(pl.multiple_of(g * 256 + i * 32, 32), 32)
            normed[rows, :] = (s * gain[...].astype(F32)).astype(BF)
            cotm[rows, :] = ct[k, g, pl.ds(f, 4)].astype(F32).reshape(32, 2048).astype(BF)

    def project(g, i):
        rows = pl.ds(g * 256, 256)
        if i < 3:
            proj[i] = nn(normed[rows, :], w[i].reshape(2048, 512)).astype(BF)
        else:
            proj[3] = nt(cotm[rows, :], wom[...]).astype(BF)

    def attention(g):
        @pl.loop(0, 4)
        def _(h):
            cols = pl.ds(pl.multiple_of(h * 128, 128), 128)
            for clip in range(2):
                rows = pl.ds(clip * 128, 128)
                out = pl.ds(g * 256 + clip * 128, 128)
                q, k, v, u = (proj[j, rows, cols] for j in range(4))
                s = nt(q, k) * FACTOR + mask[...]
                e = jnp.exp(s - jnp.max(s, axis=-1, keepdims=True))
                p = e / jnp.sum(e, axis=-1, keepdims=True)
                p_b = p.astype(BF)
                back[3, out, cols] = nn(p_b, v).astype(BF)
                d = nt(u, v)
                ds = (p * (d - jnp.sum(p * d, axis=-1, keepdims=True))).astype(BF)
                back[0, out, cols] = (nn(ds, k) * FACTOR).astype(BF)
                back[1, out, cols] = (tn(ds, q) * FACTOR).astype(BF)
                back[2, out, cols] = tn(p_b, u).astype(BF)

    swapped = {}

    def partials(g):
        rows = pl.ds(g * 256, 256)
        for h in range(2):
            half = pl.ds(h * 1024, 1024)
            mp[g, :, :, :, half] = nn(back[3, rows, :], wom[:, half]).reshape(2, 16, 8, 1024).astype(BF)
            dn = None
            for i in range(3):
                term = nt(back[i, rows, :], w[i, pl.ds(2 * h, 2)].reshape(1024, 512))
                dn = term if dn is None else dn + term
            dp[g, :, :, :, half] = dn.reshape(2, 16, 8, 1024).astype(BF)
            total = jnp.sum(dn * scaled[:, half], axis=0, keepdims=True)
            gg[:, half] = total if g == 0 else gg[:, half] + total
        swapped[g] = []
        for j, (src, dst) in enumerate([(mp, mr), (dp, dr)]):
            copy = rcopy(src.at[g, 1 - c], dst.at[g], (sw_s, sw_r), 2 * g + j, sib)
            copy.start()
            swapped[g].append(copy)

    def finalize(g):
        for j, staged in enumerate((om, og)):
            wait_bytes(staged.at[g, pl.ds(0, 15)], in_s.at[2 * g + j])
        for copy in swapped[g]:
            copy.wait_recv()

        @pl.loop(0, 4)
        def _(i):
            fs = pl.ds(i * 4, 4)
            value = t[c, g, fs].astype(F32)
            om[g, fs] = (value + (mp[g, c, fs].astype(F32) + mr[g, fs].astype(F32))).astype(BF)
            centered = value - jnp.mean(value, axis=-1, keepdims=True)
            inverse = lax.rsqrt(jnp.mean(centered * centered, axis=-1, keepdims=True) + 1e-05)
            s = centered * inverse
            ds = (dp[g, c, fs].astype(F32) + dr[g, fs].astype(F32)) * gain[...].astype(F32).reshape(1, 1, 2048)
            first = jnp.mean(ds, axis=-1, keepdims=True)
            second = jnp.mean(ds * s, axis=-1, keepdims=True)
            og[g, fs] = (inverse * (ds - first - s * second) + ct[c, g, fs].astype(F32)).astype(BF)

        for dz, dx in OFFSETS:
            zz, xx = up(z, dz), up(x, dx)
            for j, (src, dst) in enumerate([(om, mixed), (og, grad)]):
                rcopy(src.at[g, zz * 4 + xx], dst.at[tm, g], (bk_s, bk_r), j, device(y, c, zz, xx)).start()
        for j, (src, dst) in enumerate([(om, mixed), (og, grad)]):
            pltpu.make_async_copy(src.at[g, tm], dst.at[tm, g], bk_r.at[j]).start()

    def w_terms(i):
        @pl.loop(0, 8)
        def _(b):
            cols = pl.ds(pl.multiple_of(b * 256, 256), 256)
            w[i, lax.div(b, 2), lax.rem(b, 2)] = tn(normed[:, cols], back[i]).reshape(4, 4, 16, 512).astype(BF)

    def o_terms():
        @pl.loop(0, 2)
        def _(b):
            cols = pl.ds(pl.multiple_of(b * 256, 256), 256)
            wo[pl.ds(2 * b, 2)] = tn(back[3, :, cols], cotm[...]).reshape(2, 4, 4, 8, 2048).astype(BF)

    rs = (rs_s, rs_r)

    def term_ring(i, part, place, p):
        return RingSum(part, place, p, rs, 12 * i, via1.at[i], land1.at[i], lambda h: sum1.at[i, h])

    def term_sums(i, part2, place2, p2, place3, p3_):
        second = DirectSum(part2, place2, p2, rs, 12 * i + 6, land2.at[i], sum2.at[i])
        third = DirectSum(lambda v: sum2.at[i, :, v], place3, p3_, rs, 12 * i + 9, land3.at[i], p3.at[i])
        return second, third

    qx = term_ring(0, lambda v, h: w.at[0, v, h], at_y, y)
    qy, qz = term_sums(0, lambda v: sum1.at[0, :, v], at_z, z, at_x, x)
    kx = term_ring(1, lambda v, h: w.at[1, :, h, :, v], at_x, x)
    ky, kz = term_sums(1, lambda v: sum1.at[1, :, v], at_y, y, at_z, z)
    vx = term_ring(2, lambda v, h: w.at[2, :, h, v], at_z, z)
    vy, vz = term_sums(2, lambda v: sum1.at[2, :, :, v], at_x, x, at_y, y)
    dx = RingSum(lambda v, h: wo.at[v, pl.ds(2 * h, 2), :, :, o0], at_y, y, rs, 36, dvia, dland, lambda h: d1.at[pl.ds(2 * h, 2)])
    dy = DirectSum(lambda v: d1.at[:, v], at_x, x, rs, 42, dland2, d2)
    dz = DirectSum(lambda v: d2.at[pl.ds(v, 1)], at_z, z, rs, 45, dland3, q3.at[:, :, o0])
    ex = RingSum(lambda v, h: wo.at[pl.ds(2 * h, 2), :, v, :, o1], at_x, x, rs, 48, evia, eland, lambda h: e1.at[pl.ds(2 * h, 2)])
    ey = DirectSum(lambda v: e1.at[:, v], at_z, z, rs, 54, eland2, e2)
    ez = DirectSum(lambda v: e2.at[pl.ds(v, 1)], at_y, y, rs, 57, eland3, q3.at[:, :, o1])
    fx = RingSum(lambda v, h: wo.at[pl.ds(2 * h, 2), v, :, :, o2], at_z, z, rs, 60, fvia, fland, lambda h: f1.at[pl.ds(2 * h, 2)])
    fy = DirectSum(lambda v: f1.at[v], at_y, y, rs, 66, fland2, f2)
    fz = DirectSum(lambda v: f2.at[pl.ds(v, 1)], at_x, x, rs, 69, fland3, q3.at[:, :, o2])
    all_sums = (qx, qy, qz, kx, ky, kz, vx, vy, vz, dx, dy, dz, ex, ey, ez, fx, fy, fz)

    def gain_start(k, src):
        place, p = [(at_y, y), (at_z, z), (at_x, x)][k]
        out = []
        for d in (1, 2, 3):
            copy = rcopy(src, gland.at[3 * k + d - 1], (gn_s, gn_r), 3 * k + d - 1, place(up(p, d)))
            copy.start()
            out.append(copy)
        return out

    def gain_finish(k, src, copies):
        for copy in copies:
            copy.wait_recv()
        gacc[k] = src[...] + gland[3 * k] + gland[3 * k + 1] + gland[3 * k + 2]

    own_o.wait()
    for r in (da, ea, fa):
        r.start()
    for copy in own_w:
        copy.wait()
    for copy in swap_w:
        copy.wait_recv()
    for r in (qa, ka, va):
        r.start()
    rows_i = lax.broadcasted_iota(jnp.int32, (128, 128), 0)
    cols_i = lax.broadcasted_iota(jnp.int32, (128, 128), 1)
    same = lax.rem(rows_i + 128 - cols_i, 8) == 0
    mask[...] = jnp.where(same & (cols_i <= rows_i), 0.0, -1e30)
    for a, b in zip(firsts, seconds):
        a.arrive()
        b.start()
    for a, b in zip(seconds, thirds):
        a.arrive()
        b.start()
    spread(0)
    for r in thirds:
        r.relay()
    spread(1)
    pass_on(0)
    norm(0)
    qc.arrive()
    project(0, 0)
    vc.arrive()
    project(0, 2)
    spread(2)
    for r in (dc, ec, fc):
        r.arrive()

    @pl.loop(0, 4)
    def _(j):
        wom[pl.ds(pl.multiple_of(j * 128, 128), 128), :] = wo[j].astype(F32).reshape(128, 2048).astype(BF)

    project(0, 3)
    kc.arrive()
    project(0, 1)
    attention(0)
    pass_on(1)
    partials(0)
    norm(1)
    for i in range(4):
        project(1, i)
    finalize(0)
    attention(1)
    pass_on(2)
    partials(1)
    norm(2)
    for i in range(4):
        project(2, i)
    finalize(1)
    attention(2)
    partials(2)
    for i in range(16):
        gland[9, pl.ds(i, 1), :] = gg[:, pl.ds(128 * i, 128)]
    g0 = gain_start(0, gland.at[9])
    for r in rings:
        r.finish()
    o_terms()
    for r in (dx, ex, fx):
        r.start()
    w_terms(0)
    qx.start()
    w_terms(1)
    kx.start()
    finalize(2)
    w_terms(2)
    vx.start()
    for r in (dx, ex, fx):
        r.relay()
    qx.relay()
    kx.relay()
    gain_finish(0, gland.at[9], g0)
    g1 = gain_start(1, gacc.at[0])
    vx.relay()
    for a, b in ((dx, dy), (ex, ey), (fx, fy)):
        a.finish()
        b.start()
    for a, b in ((qx, qy), (kx, ky)):
        a.finish()
        b.start()
    gain_finish(1, gacc.at[0], g1)
    g2 = gain_start(2, gacc.at[1])
    vx.finish()
    vy.start()
    for a, b in ((dy, dz), (ey, ez), (fy, fz), (qy, qz), (ky, kz), (vy, vz)):
        a.finish()
        b.start()
    gain_finish(2, gacc.at[1], g2)
    g3 = rcopy(gacc.at[2], gland.at[10], (gn_s, gn_r), 9, sib)
    g3.start()
    last = {}

    def across(i):
        copy = rcopy(p3.at[i, 1 - c], p3r.at[i], (sw_s, sw_r), 6 + i, sib)
        copy.start()
        last[i] = copy

    def put(i, out):
        last[i].wait_recv()
        for j in range(4):
            cols = pl.ds(128 * j, 128)
            out[:, pl.ds(pl.multiple_of((2 * j + c) * 128, 128), 128)] = p3[i, c, :, cols]
            out[:, pl.ds(pl.multiple_of((2 * j + 1 - c) * 128, 128), 128)] = p3r[i, :, cols]

    for r in (dz, ez, fz):
        r.finish()
    for i, r in enumerate((qz, kz, vz)):
        r.finish()
        across(i)
    g_o[...] = q3[0]
    g3.wait_recv()
    gsum[...] = gacc[2] + gland[10]
    put(0, g_q)
    put(1, g_k)
    put(2, g_v)
    for j, (src, dst) in enumerate([(om, mixed), (og, grad)]):
        wait_bytes(dst, bk_r.at[j])
        wait_bytes(src.at[:, pl.ds(0, 15)], bk_s.at[j])
    for copies in (swap_w, passed[0], passed[1], passed[2], swapped[0], swapped[1], swapped[2], g0, g1, g2, [g3], list(last.values())):
        for copy in copies:
            copy.wait_send()
    for r in all_sums:
        r.drain()


def block_call(tok, cot, wq, wk, wv, w_out, gain):
    vm = pl.BlockSpec(memory_space=pltpu.VMEM)
    any_ = pl.BlockSpec(memory_space=pl.ANY)
    sds = jax.ShapeDtypeStruct
    V = pltpu.VMEM
    sem = pltpu.SemaphoreType.DMA
    rows = (16, 3, 8, 2048)
    groups = (3, 16, 8, 2048)

    def ring(lead, unit):
        return [V(lead + (4,) + unit, BF), V(lead + (2, 2) + unit, BF)]

    def out_sums(n):
        return ring((), (2, 4, 8, n)) + [V(u, BF) for u in ((4, 4, 8, n), (3, 4, 8, n), (4, 8, n), (3, 1, 8, n))]

    sems = [60, 60, 12, 12, 12, 6, 6, 6, 6, 9, 9, 2, 2, 72, 72, 10, 10, 7]
    return pl.pallas_call(
        block_kernel,
        out_shape=(sds(rows, BF), sds(rows, BF))
        + (sds((16, 1024), F32),) * 3
        + (sds((8, 2048), F32), sds((16, 128), F32)),
        in_specs=[any_] * 6 + [vm],
        out_specs=(any_, any_) + (vm,) * 5,
        scratch_shapes=[V((2, 3, 16, 8, 2048), BF)] * 2
        + [V((3, 4, 2, 4, 4, 16, 512), BF), V((4, 4, 4, 8, 2048), BF), V((512, 2048), BF)]
        + [V((768, 2048), BF)] * 2
        + [V((256, 2048), F32), V((4, 256, 512), BF), V((4, 768, 512), BF), V((128, 128), F32)]
        + [V((3, 2, 16, 8, 2048), BF)] * 2
        + [V(groups, BF)] * 4
        + ring((3,), (4, 4, 16, 512))
        + [V((3, 2, 4, 4, 16, 512), BF)]
        + [V((3, 3, 2, 4, 16, 512), BF)]
        + [V((3, 2, 4, 16, 512), BF)]
        + [V((3, 3, 2, 16, 512), BF)]
        + [V((3, 2, 16, 512), F32), V((3, 16, 512), F32)]
        + out_sums(CUT)
        + out_sums((2048 - CUT) // 2)
        + out_sums((2048 - CUT) // 2)
        + [V((1, 8, 2048), F32)]
        + [V((1, 2048), F32), V((11, 16, 128), F32), V((3, 16, 128), F32)]
        + [sem((n,)) for n in sems],
        compiler_params=pltpu.CompilerParams(collective_id=0, has_side_effects=True, vmem_limit_bytes=VMEM_LIMIT),
        name="block",
    )(tok, cot, wq, wk, wv, w_out, gain)


def finish_kernel(*refs):
    ins, outs, gsum, gain_out, held, sems = refs[:6], refs[7:13], refs[6], refs[13], refs[14:20], refs[20]
    pieces = [(i, pl.ds(4 * k, 4)) for i in range(2) for k in range(4)] + [(i, slice(None)) for i in range(2, 6)]
    enter = [pltpu.make_async_copy(ins[i].at[at], held[i].at[at], sems.at[n]) for n, (i, at) in enumerate(pieces)]
    leave = [pltpu.make_async_copy(held[i].at[at], outs[i].at[at], sems.at[12 + n]) for n, (i, at) in enumerate(pieces)]
    for copy in enter:
        copy.start()
    index = lax.axis_index("dp") * 16 + lax.axis_index("tm")
    row = gsum[pl.ds(lax.div(index, 8), 1), :]
    out = jnp.zeros((1, 16), F32)
    for i in range(8):
        out = jnp.where(lax.rem(index, 8) == i, row[:, 16 * i : 16 * i + 16], out)
    gain_out[...] = out
    for before, after in zip(enter, leave):
        before.wait()
        after.start()
    for copy in leave:
        copy.wait()


def finish_call(arrays, gsum):
    vm = pl.BlockSpec(memory_space=pltpu.VMEM)
    any_ = pl.BlockSpec(memory_space=pl.ANY)
    return pl.pallas_call(
        finish_kernel,
        out_shape=tuple(jax.ShapeDtypeStruct(a.shape, a.dtype) for a in arrays) + (jax.ShapeDtypeStruct((1, 16), F32),),
        in_specs=[any_] * 6 + [vm],
        out_specs=(any_,) * 6 + (vm,),
        scratch_shapes=[pltpu.VMEM(a.shape, a.dtype) for a in arrays] + [pltpu.SemaphoreType.DMA((24,))],
        name="finish",
    )(*arrays, gsum)


def on_device(tokens, cotangent, norm_gain, w_query, w_key, w_value, w_out):
    tok = tokens.reshape(16, 3, 8, 2048)
    cot = cotangent.reshape(16, 3, 8, 2048)
    gain = norm_gain.reshape(1, 2048)
    *arrays, gsum = block_call(tok, cot, w_query, w_key, w_value, w_out, gain)
    mixed, grad, g_q, g_k, g_v, g_o, grad_gain = finish_call(arrays, gsum)
    shape = (1, 1, 384, 2048)
    return mixed.reshape(shape), grad.reshape(shape), grad_gain.reshape(16), g_q, g_k, g_v, g_o


def solution(mesh):
    rows = P("dp", "tm", None, None)
    weight = P(("dp", "tm"), None)
    return jax.shard_map(
        on_device,
        mesh=mesh,
        in_specs=(rows, rows, P()) + (weight,) * 4,
        out_specs=(rows, rows, P(("dp", "tm"))) + (weight,) * 4,
        check_vma=False,
    )
```

```python
import functools

import jax
import jax.numpy as jnp
from jax import lax
from jax.experimental import pallas as pl
from jax.experimental.pallas import tpu as pltpu
from jax.sharding import PartitionSpec as P

MESH = pl.DeviceIdType.MESH
CUT = 1024
VMEM_LIMIT = 62 * 1024 * 1024


def coords():
    dp, tm = lax.axis_index("dp"), lax.axis_index("tm")
    return lax.div(dp, 2), lax.rem(dp, 2), lax.div(tm, 4), lax.rem(tm, 4)


def device(y, c, z, x):
    return {"dp": y * 2 + c, "tm": z * 4 + x}


def up(p, d):
    return lax.rem(p + d, 4)


def rcopy(src, dst, sems, i, where):
    return pltpu.make_async_remote_copy(
        src_ref=src,
        dst_ref=dst,
        send_sem=sems[0].at[i],
        recv_sem=sems[1].at[i],
        device_id=where,
        device_id_type=MESH,
    )


OFFSETS = [
    (0, 1), (0, 3), (1, 0), (3, 0), (1, 1), (3, 3), (1, 3), (3, 1),
    (2, 2), (0, 2), (2, 0), (2, 1), (2, 3), (1, 2), (3, 2),
]


def greet(y, c, z, x, tm_peers=True):
    barrier = pltpu.get_barrier_semaphore()
    peers = [device(y, 1 - c, z, x)] + [device(up(y, d), c, z, x) for d in (1, 2, 3)]
    peers += [device(y, c, up(z, dz), up(x, dx)) for dz, dx in OFFSETS]
    for peer in peers:
        pl.semaphore_signal(barrier, inc=1, device_id=peer, device_id_type=MESH)
    pl.semaphore_wait(barrier, len(peers))


class Ring:
    def __init__(self, block, half, place, p, sems, first):
        self.block, self.half, self.place, self.p = block, half, place, p
        self.sems, self.first = sems, first

    def start(self):
        p, b = self.p, self.block(self.p)
        self.right = rcopy(b, b, self.sems, self.first, self.place(up(p, 1)))
        self.left = rcopy(b, b, self.sems, self.first + 1, self.place(up(p, 3)))
        self.right.start()
        self.left.start()

    def relay(self):
        p = self.p
        self.right.wait_recv()
        h = self.half(up(p, 3), 0)
        self.on_right = rcopy(h, h, self.sems, self.first + 2, self.place(up(p, 1)))
        self.on_right.start()
        self.left.wait_recv()
        h = self.half(up(p, 1), 1)
        self.on_left = rcopy(h, h, self.sems, self.first + 3, self.place(up(p, 3)))
        self.on_left.start()

    def arrive(self):
        self.on_right.wait_recv()
        self.on_left.wait_recv()

    def finish(self):
        for copy in (self.right, self.left, self.on_right, self.on_left):
            copy.wait_send()


class Direct:
    def __init__(self, block, place, p, sems, first):
        b = block(p)
        self.copies = [rcopy(b, b, sems, first + d - 1, place(up(p, d))) for d in (1, 2, 3)]

    def start(self):
        for copy in self.copies:
            copy.start()

    def arrive(self):
        for copy in self.copies:
            copy.wait_recv()

    def finish(self):
        for copy in self.copies:
            copy.wait_send()


def nt(a, b):
    return lax.dot_general(a, b, (((1,), (1,)), ((), ())), preferred_element_type=jnp.float32)


def tn(a, b):
    return lax.dot_general(a, b, (((0,), (0,)), ((), ())), preferred_element_type=jnp.float32)


def nn(a, b):
    return jnp.dot(a, b, preferred_element_type=jnp.float32)


FACTOR = 128 ** (-0.5)
BF = jnp.bfloat16
F32 = jnp.float32


def add(out, terms):
    @pl.loop(0, out.shape[0])
    def _(i):
        value = terms[0][i].astype(F32)
        for term in terms[1:]:
            value = value + term[i].astype(F32)
        out[i] = value.astype(out.dtype)


class DirectSum:
    def __init__(self, part, place, p, sems, first, land, total):
        self.own, self.land, self.total = part(p), land, total
        self.copies = [rcopy(part(up(p, d)), land.at[d - 1], sems, first + d - 1, place(up(p, d))) for d in (1, 2, 3)]

    def start(self):
        for copy in self.copies:
            copy.start()

    def finish(self):
        for copy in self.copies:
            copy.wait_recv()
        add(self.total, [self.own] + [self.land.at[d] for d in range(3)])

    def drain(self):
        for copy in self.copies:
            copy.wait_send()


class RingSum:
    def __init__(self, part, place, p, sems, first, via, land, total):
        self.part, self.place, self.p, self.sems, self.first = part, place, p, sems, first
        self.via, self.land, self.total = via, land, total

    def copy(self, i, src, dst, step):
        c = rcopy(src, dst, self.sems, self.first + i, self.place(up(self.p, step)))
        c.start()
        return c

    def start(self):
        p = self.p
        self.a = self.copy(0, self.part(up(p, 2), 0), self.via.at[0], 1)
        self.b = self.copy(1, self.part(up(p, 2), 1), self.via.at[1], 3)
        self.d = self.copy(2, self.part(up(p, 1), 1), self.land.at[0, 1], 1)
        self.e = self.copy(3, self.part(up(p, 3), 0), self.land.at[1, 0], 3)

    def relay(self):
        p = self.p
        self.a.wait_recv()
        add(self.via.at[2], [self.via.at[0], self.part(up(p, 1), 0)])
        self.f = self.copy(4, self.via.at[2], self.land.at[0, 0], 1)
        self.b.wait_recv()
        add(self.via.at[3], [self.via.at[1], self.part(up(p, 3), 1)])
        self.g = self.copy(5, self.via.at[3], self.land.at[1, 1], 3)

    def finish(self):
        for c in (self.d, self.e, self.f, self.g):
            c.wait_recv()
        for h in range(2):
            add(self.total(h), [self.part(self.p, h), self.land.at[0, h], self.land.at[1, h]])

    def drain(self):
        for c in (self.a, self.b, self.d, self.e, self.f, self.g):
            c.wait_send()


def wait_bytes(ref, sem):
    pltpu.make_async_copy(ref, ref, sem).wait()


def block_kernel(tok, cot, wq, wk, wv, w_out, gain, mixed, grad, g_q, g_k, g_v, g_o, gsum,
                 t, cth, w, wo, wom, normed, cotm, scaled, proj, ups, upt, back, atts, atth, attm, mask,
                 mrh, dp, dr, om, og, gh,
                 via1, land1, sum1, land2, sum2, land3, p3, p3r,
                 dvia, dland, d1, dland2, d2, dland3, evia, eland, e1, eland2, e2, eland3,
                 fvia, fland, f1, fland2, f2, fland3, q3,
                 gg, gland, gacc,
                 ag_s, ag_r, w_s, w_r, w_l, in_s, in_r, fw_s, fw_r, c_s, c_r, up_s, up_r, at_s, at_r, sw_s, sw_r,
                 bk_s, bk_r, rs_s, rs_r, gn_s, gn_r, loc, out_l):
    y, c, z, x = coords()
    tm = z * 4 + x
    sib = device(y, 1 - c, z, x)
    at_x = lambda v: device(y, c, z, v)
    at_y = lambda v: device(v, c, z, x)
    at_z = lambda v: device(y, c, v, x)
    mph = cth

    stage, cot_own = [], []
    for g in range(3):
        copy = pltpu.make_async_copy(tok.at[:, g], om.at[g], loc.at[g])
        copy.start()
        stage.append(copy)
    own_o = pltpu.make_async_copy(w_out, wo.at[y, z, x], loc.at[6])
    own_o.start()
    own_w = []
    for i, src in enumerate((wq, wk, wv)):
        for j in range(4):
            cols = pl.ds(pl.multiple_of((2 * j + c) * 128, 128), 128)
            copy = pltpu.make_async_copy(src.at[:, cols], w.at[i, y, c, z, x, :, pl.ds(128 * j, 128)], w_l.at[4 * i + j])
            copy.start()
            own_w.append(copy)
    for g in range(3):
        copy = pltpu.make_async_copy(cot.at[:, g], cth.at[g, c], loc.at[3 + g])
        copy.start()
        cot_own.append(copy)
    greet(y, c, z, x)

    swap_w = []
    for i, src in enumerate((wq, wk, wv)):
        for j in range(4):
            cols = pl.ds(pl.multiple_of((2 * j + 1 - c) * 128, 128), 128)
            copy = rcopy(src.at[:, cols], w.at[i, y, c, z, x, :, pl.ds(128 * j, 128)], (w_s, w_r), 4 * i + j, sib)
            copy.start()
            swap_w.append(copy)
    swap_c = []
    for g in range(3):
        cot_own[g].wait()
        copy = rcopy(cth.at[g, c], cth.at[g, c], (c_s, c_r), g, sib)
        copy.start()
        swap_c.append(copy)

    ag = (ag_s, ag_r)
    qa = Direct(lambda v: w.at[0, y, :, z, v], at_x, x, ag, 0)
    qb = Direct(lambda v: w.at[0, y, :, v], at_z, z, ag, 3)
    qc = Ring(lambda v: w.at[0, v], lambda v, k: w.at[0, v, k], at_y, y, ag, 6)
    ka = Direct(lambda v: w.at[1, y, :, v, x], at_z, z, ag, 10)
    kb = Direct(lambda v: w.at[1, v, :, :, x], at_y, y, ag, 13)
    kc = Ring(lambda v: w.at[1, :, :, :, v], lambda v, k: w.at[1, :, k, :, v], at_x, x, ag, 16)
    va = Direct(lambda v: w.at[2, v, :, z, x], at_y, y, ag, 20)
    vb = Direct(lambda v: w.at[2, :, :, z, v], at_x, x, ag, 23)
    vc = Ring(lambda v: w.at[2, :, :, v], lambda v, k: w.at[2, :, k, v], at_z, z, ag, 26)
    o0, o1, o2 = (pl.ds(0, CUT), pl.ds(CUT, (2048 - CUT) // 2), pl.ds(CUT + (2048 - CUT) // 2, (2048 - CUT) // 2))
    da = Direct(lambda v: wo.at[y, v, x, :, o0], at_z, z, ag, 30)
    db = Direct(lambda v: wo.at[y, :, v, :, o0], at_x, x, ag, 33)
    dc = Ring(lambda v: wo.at[v, :, :, :, o0], lambda v, k: wo.at[v, pl.ds(2 * k, 2), :, :, o0], at_y, y, ag, 36)
    ea = Direct(lambda v: wo.at[v, z, x, :, o1], at_y, y, ag, 40)
    eb = Direct(lambda v: wo.at[:, v, x, :, o1], at_z, z, ag, 43)
    ec = Ring(lambda v: wo.at[:, :, v, :, o1], lambda v, k: wo.at[pl.ds(2 * k, 2), :, v, :, o1], at_x, x, ag, 46)
    fa = Direct(lambda v: wo.at[y, z, v, :, o2], at_x, x, ag, 50)
    fb = Direct(lambda v: wo.at[v, z, :, :, o2], at_y, y, ag, 53)
    fc = Ring(lambda v: wo.at[:, v, :, :, o2], lambda v, k: wo.at[pl.ds(2 * k, 2), v, :, :, o2], at_z, z, ag, 56)
    firsts, seconds, thirds = (qa, ka, va, da, ea, fa), (qb, kb, vb, db, eb, fb), (qc, kc, vc, dc, ec, fc)
    rings = firsts + seconds + thirds

    def to_all(send):
        for dz, dx in OFFSETS:
            zz, xx = up(z, dz), up(x, dx)
            send(zz * 4 + xx, device(y, c, zz, xx))

    def spread(g):
        stage[g].wait()
        pltpu.make_async_copy(tok.at[tm, g], t.at[c, g, tm], in_r.at[g]).start()
        to_all(lambda j, place: rcopy(om.at[g, j], t.at[c, g, tm], (in_s, in_r), g, place).start())

    passed = {}

    def pass_on(g):
        wait_bytes(t.at[c, g], in_r.at[g])
        passed[g] = rcopy(t.at[c, g], t.at[c, g], (fw_s, fw_r), g, sib)
        passed[g].start()

    def cot_rows():
        for g in range(3):
            swap_c[g].wait_recv()

            @pl.loop(0, 8)
            def _(i):
                k, f = lax.div(i, 4), lax.rem(i, 4) * 4
                rows = pl.ds(pl.multiple_of(g * 256 + i * 32, 32), 32)
                cotm[rows, :] = cth[g, k, pl.ds(f, 4)].astype(F32).reshape(32, 2048).astype(BF)

    def wo_rows():
        @pl.loop(0, 4)
        def _(j):
            wom[pl.ds(pl.multiple_of(j * 128, 128), 128), :] = wo[j].astype(F32).reshape(128, 2048).astype(BF)

    def upstream():
        @pl.loop(0, 3)
        def _(g):
            rows = pl.ds(pl.multiple_of(g * 256, 256), 256)
            ups[g] = nt(cotm[rows, :], wom[...]).reshape(2, 16, 8, 512).astype(BF)

        pltpu.make_async_copy(ups.at[:, :, tm], upt.at[:, :, tm], up_r.at[0]).start()
        to_all(lambda j, place: rcopy(ups.at[:, :, j], upt.at[:, :, tm], (up_s, up_r), 0, place).start())

    def norm(g):
        passed[g].wait_recv()

        @pl.loop(0, 8)
        def _(i):
            k, f = lax.div(i, 4), lax.rem(i, 4) * 4
            value = t[k, g, pl.ds(f, 4)].astype(F32).reshape(32, 2048)
            centered = value - jnp.mean(value, axis=-1, keepdims=True)
            inverse = lax.rsqrt(jnp.mean(centered * centered, axis=-1, keepdims=True) + 1e-05)
            s = centered * inverse
            scaled[pl.ds(pl.multiple_of(i * 32, 32), 32), :] = s
            rows = pl.ds(pl.multiple_of(g * 256 + i * 32, 32), 32)
            normed[rows, :] = (s * gain[...].astype(F32)).astype(BF)

    def project(g, i):
        rows = pl.ds(g * 256, 256)
        if i < 3:
            proj[i] = nn(normed[rows, :], w[i].reshape(2048, 512)).astype(BF)
        else:
            proj[3] = upt[g].astype(F32).reshape(256, 512).astype(BF)

    def attention(g):
        @pl.loop(0, 4)
        def _(h):
            cols = pl.ds(pl.multiple_of(h * 128, 128), 128)
            for clip in range(2):
                rows = pl.ds(clip * 128, 128)
                out = pl.ds(g * 256 + clip * 128, 128)
                q, k, v, u = (proj[j, rows, cols] for j in range(4))
                s = nt(q, k) * FACTOR + mask[...]
                e = jnp.exp(s - jnp.max(s, axis=-1, keepdims=True))
                p = e / jnp.sum(e, axis=-1, keepdims=True)
                p_b = p.astype(BF)
                atts[g, clip, :, :, cols] = nn(p_b, v).reshape(16, 8, 128).astype(BF)
                d = nt(u, v)
                ds = (p * (d - jnp.sum(p * d, axis=-1, keepdims=True))).astype(BF)
                back[0, out, cols] = (nn(ds, k) * FACTOR).astype(BF)
                back[1, out, cols] = (tn(ds, q) * FACTOR).astype(BF)
                back[2, out, cols] = tn(p_b, u).astype(BF)

        pltpu.make_async_copy(atts.at[g, :, tm], atth.at[g, :, tm], at_r.at[g]).start()
        to_all(lambda f, place: rcopy(atts.at[g, :, f], atth.at[g, :, tm], (at_s, at_r), g, place).start())

    swapped = {}

    def partials(g):
        rows = pl.ds(g * 256, 256)
        for h in range(2):
            half = pl.ds(h * 1024, 1024)
            dn = None
            for i in range(3):
                term = nt(back[i, rows, :], w[i, pl.ds(2 * h, 2)].reshape(1024, 512))
                dn = term if dn is None else dn + term
            dp[g, :, :, :, half] = dn.reshape(2, 16, 8, 1024).astype(BF)
            total = jnp.sum(dn * scaled[:, half], axis=0, keepdims=True)
            gg[:, half] = total if g == 0 else gg[:, half] + total
        swapped[g] = rcopy(dp.at[g, 1 - c], dr.at[g], (sw_s, sw_r), g, sib)
        swapped[g].start()

    def finalize(g):
        swapped[g].wait_recv()

        @pl.loop(0, 4)
        def _(i):
            fs = pl.ds(i * 4, 4)
            value = t[c, g, fs].astype(F32)
            centered = value - jnp.mean(value, axis=-1, keepdims=True)
            inverse = lax.rsqrt(jnp.mean(centered * centered, axis=-1, keepdims=True) + 1e-05)
            s = centered * inverse
            ds = (dp[g, c, fs].astype(F32) + dr[g, fs].astype(F32)) * gain[...].astype(F32).reshape(1, 1, 2048)
            first = jnp.mean(ds, axis=-1, keepdims=True)
            second = jnp.mean(ds * s, axis=-1, keepdims=True)
            og[g, fs] = (inverse * (ds - first - s * second)).astype(BF)

        pltpu.make_async_copy(og.at[g, tm], gh.at[g, tm], bk_r.at[g]).start()
        to_all(lambda f, place: rcopy(og.at[g, f], gh.at[g, tm], (bk_s, bk_r), g, place).start())

    mixed_swap, written = {}, []

    def home_rows(g):
        wait_bytes(atth.at[g], at_r.at[g])
        attm[pl.ds(g * 256, 256), :] = atth[g].astype(F32).reshape(256, 512).astype(BF)

    def home(g):
        rows = pl.ds(g * 256, 256)
        for h in range(2):
            half = pl.ds(h * 1024, 1024)
            mph[g, :, :, :, half] = nn(attm[rows, :], wom[:, half]).reshape(2, 16, 8, 1024).astype(BF)
        mixed_swap[g] = rcopy(mph.at[g, 1 - c], mrh.at[g], (sw_s, sw_r), 3 + g, sib)
        mixed_swap[g].start()

    def write(g, j, src, dst):
        copy = pltpu.make_async_copy(src.at[g], dst.at[:, g], out_l.at[2 * g + j])
        copy.start()
        written.append(copy)

    def mixed_out(g):
        wait_bytes(om.at[g, pl.ds(0, 15)], in_s.at[g])
        mixed_swap[g].wait_recv()

        @pl.loop(0, 4)
        def _(i):
            js = pl.ds(i * 4, 4)
            om[g, js] = (om[g, js].astype(F32) + (mph[g, c, js].astype(F32) + mrh[g, js].astype(F32))).astype(BF)

        write(g, 0, om, mixed)

    def grad_out(g):
        wait_bytes(gh.at[g], bk_r.at[g])

        @pl.loop(0, 4)
        def _(i):
            js = pl.ds(i * 4, 4)
            rows = pl.ds(pl.multiple_of(g * 256 + c * 128 + i * 32, 32), 32)
            gh[g, js] = (gh[g, js].astype(F32) + cotm[rows, :].astype(F32).reshape(4, 8, 2048)).astype(BF)

        write(g, 1, gh, grad)

    def w_terms(i):
        @pl.loop(0, 8)
        def _(b):
            cols = pl.ds(pl.multiple_of(b * 256, 256), 256)
            w[i, lax.div(b, 2), lax.rem(b, 2)] = tn(normed[:, cols], back[i]).reshape(4, 4, 16, 512).astype(BF)

    def o_terms():
        @pl.loop(0, 2)
        def _(b):
            cols = pl.ds(pl.multiple_of(b * 256, 256), 256)
            wo[pl.ds(2 * b, 2)] = tn(attm[:, cols], cotm[...]).reshape(2, 4, 4, 8, 2048).astype(BF)

    rs = (rs_s, rs_r)

    def term_ring(i, part, place, p):
        return RingSum(part, place, p, rs, 12 * i, via1.at[i], land1.at[i], lambda h: sum1.at[i, h])

    def term_sums(i, part2, place2, p2, place3, p3_):
        second = DirectSum(part2, place2, p2, rs, 12 * i + 6, land2.at[i], sum2.at[i])
        third = DirectSum(lambda v: sum2.at[i, :, v], place3, p3_, rs, 12 * i + 9, land3.at[i], p3.at[i])
        return second, third

    qx = term_ring(0, lambda v, h: w.at[0, v, h], at_y, y)
    qy, qz = term_sums(0, lambda v: sum1.at[0, :, v], at_z, z, at_x, x)
    kx = term_ring(1, lambda v, h: w.at[1, :, h, :, v], at_x, x)
    ky, kz = term_sums(1, lambda v: sum1.at[1, :, v], at_y, y, at_z, z)
    vx = term_ring(2, lambda v, h: w.at[2, :, h, v], at_z, z)
    vy, vz = term_sums(2, lambda v: sum1.at[2, :, :, v], at_x, x, at_y, y)
    dx = RingSum(lambda v, h: wo.at[v, pl.ds(2 * h, 2), :, :, o0], at_y, y, rs, 36, dvia, dland, lambda h: d1.at[pl.ds(2 * h, 2)])
    dy = DirectSum(lambda v: d1.at[:, v], at_x, x, rs, 42, dland2, d2)
    dz = DirectSum(lambda v: d2.at[pl.ds(v, 1)], at_z, z, rs, 45, dland3, q3.at[:, :, o0])
    ex = RingSum(lambda v, h: wo.at[pl.ds(2 * h, 2), :, v, :, o1], at_x, x, rs, 48, evia, eland, lambda h: e1.at[pl.ds(2 * h, 2)])
    ey = DirectSum(lambda v: e1.at[:, v], at_z, z, rs, 54, eland2, e2)
    ez = DirectSum(lambda v: e2.at[pl.ds(v, 1)], at_y, y, rs, 57, eland3, q3.at[:, :, o1])
    fx = RingSum(lambda v, h: wo.at[pl.ds(2 * h, 2), v, :, :, o2], at_z, z, rs, 60, fvia, fland, lambda h: f1.at[pl.ds(2 * h, 2)])
    fy = DirectSum(lambda v: f1.at[v], at_y, y, rs, 66, fland2, f2)
    fz = DirectSum(lambda v: f2.at[pl.ds(v, 1)], at_x, x, rs, 69, fland3, q3.at[:, :, o2])
    all_sums = (qx, qy, qz, kx, ky, kz, vx, vy, vz, dx, dy, dz, ex, ey, ez, fx, fy, fz)

    def gain_start(k, src):
        place, p = [(at_y, y), (at_z, z), (at_x, x)][k]
        out = []
        for d in (1, 2, 3):
            copy = rcopy(src, gland.at[3 * k + d - 1], (gn_s, gn_r), 3 * k + d - 1, place(up(p, d)))
            copy.start()
            out.append(copy)
        return out

    def gain_finish(k, src, copies):
        for copy in copies:
            copy.wait_recv()
        gacc[k] = src[...] + gland[3 * k] + gland[3 * k + 1] + gland[3 * k + 2]

    own_o.wait()
    for r in (da, ea, fa):
        r.start()
    for copy in own_w:
        copy.wait()
    for copy in swap_w:
        copy.wait_recv()
    for r in (qa, ka, va):
        r.start()
    rows_i = lax.broadcasted_iota(jnp.int32, (128, 128), 0)
    cols_i = lax.broadcasted_iota(jnp.int32, (128, 128), 1)
    same = lax.rem(rows_i + 128 - cols_i, 8) == 0
    mask[...] = jnp.where(same & (cols_i <= rows_i), 0.0, -1e30)
    for a, b in ((da, db), (ea, eb), (fa, fb), (qa, qb), (ka, kb), (va, vb)):
        a.arrive()
        b.start()
    for a, b in ((db, dc), (eb, ec), (fb, fc), (qb, qc), (kb, kc), (vb, vc)):
        a.arrive()
        b.start()
    spread(0)
    cot_rows()
    for r in (dc, ec, fc):
        r.relay()
    for r in (qc, kc, vc):
        r.relay()
    for r in (dc, ec, fc):
        r.arrive()
    wo_rows()
    upstream()
    spread(1)
    pass_on(0)
    norm(0)
    qc.arrive()
    project(0, 0)
    vc.arrive()
    project(0, 2)
    kc.arrive()
    project(0, 1)
    spread(2)
    wait_bytes(upt, up_r.at[0])
    project(0, 3)
    attention(0)
    partials(0)
    pass_on(1)
    norm(1)
    for i in range(4):
        project(1, i)
    pass_on(2)
    finalize(0)
    attention(1)
    partials(1)
    norm(2)
    for i in range(4):
        project(2, i)
    finalize(1)
    attention(2)
    for r in rings:
        r.finish()
    for copy in swap_c:
        copy.wait_send()
    partials(2)
    w_terms(0)
    qx.start()
    home_rows(0)
    home_rows(1)
    w_terms(1)
    kx.start()
    home_rows(2)
    o_terms()
    for r in (dx, ex, fx):
        r.start()
    w_terms(2)
    vx.start()
    finalize(2)
    qx.relay()
    kx.relay()
    for r in (dx, ex, fx):
        r.relay()
    home(0)
    vx.relay()
    for i in range(16):
        gland[9, pl.ds(i, 1), :] = gg[:, pl.ds(128 * i, 128)]
    g0 = gain_start(0, gland.at[9])
    home(1)
    home(2)
    for a, b in ((qx, qy), (kx, ky), (dx, dy), (ex, ey), (fx, fy)):
        a.finish()
        b.start()
    gain_finish(0, gland.at[9], g0)
    g1 = gain_start(1, gacc.at[0])
    vx.finish()
    vy.start()
    mixed_out(0)
    mixed_out(1)
    mixed_out(2)
    grad_out(0)
    grad_out(1)
    for a, b in ((qy, qz), (ky, kz), (dy, dz), (ey, ez), (fy, fz)):
        a.finish()
        b.start()
    gain_finish(1, gacc.at[0], g1)
    g2 = gain_start(2, gacc.at[1])
    vy.finish()
    vz.start()
    grad_out(2)
    gain_finish(2, gacc.at[1], g2)
    g3 = rcopy(gacc.at[2], gland.at[10], (gn_s, gn_r), 9, sib)
    g3.start()
    last = {}

    def across(i):
        copy = rcopy(p3.at[i, 1 - c], p3r.at[i], (sw_s, sw_r), 6 + i, sib)
        copy.start()
        last[i] = copy

    def put(i, out):
        last[i].wait_recv()
        for j in range(4):
            cols = pl.ds(128 * j, 128)
            out[:, pl.ds(pl.multiple_of((2 * j + c) * 128, 128), 128)] = p3[i, c, :, cols]
            out[:, pl.ds(pl.multiple_of((2 * j + 1 - c) * 128, 128), 128)] = p3r[i, :, cols]

    for r in (dz, ez, fz):
        r.finish()
    for i, r in enumerate((qz, kz, vz)):
        r.finish()
        across(i)
    g_o[...] = q3[0]
    g3.wait_recv()
    gsum[...] = gacc[2] + gland[10]
    put(0, g_q)
    put(1, g_k)
    put(2, g_v)
    wait_bytes(ups.at[:, :, pl.ds(0, 15)], up_s.at[0])
    for g in range(3):
        wait_bytes(atts.at[g, :, pl.ds(0, 15)], at_s.at[g])
        wait_bytes(og.at[g, pl.ds(0, 15)], bk_s.at[g])
    for copy in written:
        copy.wait()
    for copies in (swap_w, passed.values(), swapped.values(), mixed_swap.values(), g0, g1, g2, [g3], last.values()):
        for copy in copies:
            copy.wait_send()
    for r in all_sums:
        r.drain()


def block_call(tok, cot, wq, wk, wv, w_out, gain):
    vm = pl.BlockSpec(memory_space=pltpu.VMEM)
    any_ = pl.BlockSpec(memory_space=pl.ANY)
    sds = jax.ShapeDtypeStruct
    V = pltpu.VMEM
    sem = pltpu.SemaphoreType.DMA
    rows = (16, 3, 8, 2048)
    groups = (3, 16, 8, 2048)

    def ring(lead, unit):
        return [V(lead + (4,) + unit, BF), V(lead + (2, 2) + unit, BF)]

    def out_sums(n):
        return ring((), (2, 4, 8, n)) + [V(u, BF) for u in ((4, 4, 8, n), (3, 4, 8, n), (4, 8, n), (3, 1, 8, n))]

    sems = [60, 60, 12, 12, 12, 3, 3, 3, 3, 3, 3, 1, 1, 3, 3, 9, 9, 3, 3, 72, 72, 10, 10, 7, 6]
    return pl.pallas_call(
        block_kernel,
        out_shape=(sds(rows, BF), sds(rows, BF))
        + (sds((16, 1024), F32),) * 3
        + (sds((8, 2048), F32), sds((16, 128), F32)),
        in_specs=[any_] * 6 + [vm],
        out_specs=(any_, any_) + (vm,) * 5,
        scratch_shapes=[V((2, 3, 16, 8, 2048), BF), V((3, 2, 16, 8, 2048), BF)]
        + [V((3, 4, 2, 4, 4, 16, 512), BF), V((4, 4, 4, 8, 2048), BF), V((512, 2048), BF)]
        + [V((768, 2048), BF)] * 2
        + [V((256, 2048), F32), V((4, 256, 512), BF)]
        + [V((3, 2, 16, 8, 512), BF)] * 2
        + [V((3, 768, 512), BF)]
        + [V((3, 2, 16, 8, 512), BF)] * 2
        + [V((768, 512), BF), V((128, 128), F32)]
        + [V(groups, BF), V((3, 2, 16, 8, 2048), BF)]
        + [V(groups, BF)] * 4
        + ring((3,), (4, 4, 16, 512))
        + [V((3, 2, 4, 4, 16, 512), BF)]
        + [V((3, 3, 2, 4, 16, 512), BF)]
        + [V((3, 2, 4, 16, 512), BF)]
        + [V((3, 3, 2, 16, 512), BF)]
        + [V((3, 2, 16, 512), F32), V((3, 16, 512), F32)]
        + out_sums(CUT)
        + out_sums((2048 - CUT) // 2)
        + out_sums((2048 - CUT) // 2)
        + [V((1, 8, 2048), F32)]
        + [V((1, 2048), F32), V((11, 16, 128), F32), V((3, 16, 128), F32)]
        + [sem((n,)) for n in sems],
        compiler_params=pltpu.CompilerParams(collective_id=0, has_side_effects=True, vmem_limit_bytes=VMEM_LIMIT),
        name="block",
    )(tok, cot, wq, wk, wv, w_out, gain)


def finish_kernel(*refs):
    ins, outs, gsum, gain_out, held, sems = refs[:6], refs[7:13], refs[6], refs[13], refs[14:20], refs[20]
    pieces = [(i, pl.ds(4 * k, 4)) for i in range(2) for k in range(4)] + [(i, slice(None)) for i in range(2, 6)]
    enter = [pltpu.make_async_copy(ins[i].at[at], held[i].at[at], sems.at[n]) for n, (i, at) in enumerate(pieces)]
    leave = [pltpu.make_async_copy(held[i].at[at], outs[i].at[at], sems.at[12 + n]) for n, (i, at) in enumerate(pieces)]
    for copy in enter:
        copy.start()
    index = lax.axis_index("dp") * 16 + lax.axis_index("tm")
    row = gsum[pl.ds(lax.div(index, 8), 1), :]
    out = jnp.zeros((1, 16), F32)
    for i in range(8):
        out = jnp.where(lax.rem(index, 8) == i, row[:, 16 * i : 16 * i + 16], out)
    gain_out[...] = out
    for before, after in zip(enter, leave):
        before.wait()
        after.start()
    for copy in leave:
        copy.wait()


def finish_call(arrays, gsum):
    vm = pl.BlockSpec(memory_space=pltpu.VMEM)
    any_ = pl.BlockSpec(memory_space=pl.ANY)
    return pl.pallas_call(
        finish_kernel,
        out_shape=tuple(jax.ShapeDtypeStruct(a.shape, a.dtype) for a in arrays) + (jax.ShapeDtypeStruct((1, 16), F32),),
        in_specs=[any_] * 6 + [vm],
        out_specs=(any_,) * 6 + (vm,),
        scratch_shapes=[pltpu.VMEM(a.shape, a.dtype) for a in arrays] + [pltpu.SemaphoreType.DMA((24,))],
        name="finish",
    )(*arrays, gsum)


def on_device(tokens, cotangent, norm_gain, w_query, w_key, w_value, w_out):
    tok = tokens.reshape(16, 3, 8, 2048)
    cot = cotangent.reshape(16, 3, 8, 2048)
    gain = norm_gain.reshape(1, 2048)
    *arrays, gsum = block_call(tok, cot, w_query, w_key, w_value, w_out, gain)
    mixed, grad, g_q, g_k, g_v, g_o, grad_gain = finish_call(arrays, gsum)
    shape = (1, 1, 384, 2048)
    return mixed.reshape(shape), grad.reshape(shape), grad_gain.reshape(16), g_q, g_k, g_v, g_o


def solution(mesh):
    rows = P("dp", "tm", None, None)
    weight = P(("dp", "tm"), None)
    return jax.shard_map(
        on_device,
        mesh=mesh,
        in_specs=(rows, rows, P()) + (weight,) * 4,
        out_specs=(rows, rows, P(("dp", "tm"))) + (weight,) * 4,
        check_vma=False,
    )
```

```python
import functools

import jax
import jax.numpy as jnp
from jax import lax
from jax.experimental import pallas as pl
from jax.experimental.pallas import tpu as pltpu
from jax.sharding import PartitionSpec as P

MESH = pl.DeviceIdType.MESH
CUT = 1024
VMEM_LIMIT = 62 * 1024 * 1024


def coords():
    dp, tm = lax.axis_index("dp"), lax.axis_index("tm")
    return lax.div(dp, 2), lax.rem(dp, 2), lax.div(tm, 4), lax.rem(tm, 4)


def device(y, c, z, x):
    return {"dp": y * 2 + c, "tm": z * 4 + x}


def up(p, d):
    return lax.rem(p + d, 4)


def rcopy(src, dst, sems, i, where):
    return pltpu.make_async_remote_copy(
        src_ref=src,
        dst_ref=dst,
        send_sem=sems[0].at[i],
        recv_sem=sems[1].at[i],
        device_id=where,
        device_id_type=MESH,
    )


OFFSETS = [
    (0, 1), (0, 3), (1, 0), (3, 0), (1, 1), (3, 3), (1, 3), (3, 1),
    (2, 2), (0, 2), (2, 0), (2, 1), (2, 3), (1, 2), (3, 2),
]


def greet(y, c, z, x, tm_peers=True):
    barrier = pltpu.get_barrier_semaphore()
    peers = [device(y, 1 - c, z, x)] + [device(up(y, d), c, z, x) for d in (1, 2, 3)]
    peers += [device(y, c, up(z, dz), up(x, dx)) for dz, dx in OFFSETS]
    for peer in peers:
        pl.semaphore_signal(barrier, inc=1, device_id=peer, device_id_type=MESH)
    pl.semaphore_wait(barrier, len(peers))


class Ring:
    def __init__(self, block, half, place, p, sems, first):
        self.block, self.half, self.place, self.p = block, half, place, p
        self.sems, self.first = sems, first

    def start(self):
        p, b = self.p, self.block(self.p)
        self.right = rcopy(b, b, self.sems, self.first, self.place(up(p, 1)))
        self.left = rcopy(b, b, self.sems, self.first + 1, self.place(up(p, 3)))
        self.right.start()
        self.left.start()

    def relay(self):
        p = self.p
        self.right.wait_recv()
        h = self.half(up(p, 3), 0)
        self.on_right = rcopy(h, h, self.sems, self.first + 2, self.place(up(p, 1)))
        self.on_right.start()
        self.left.wait_recv()
        h = self.half(up(p, 1), 1)
        self.on_left = rcopy(h, h, self.sems, self.first + 3, self.place(up(p, 3)))
        self.on_left.start()

    def arrive(self):
        self.on_right.wait_recv()
        self.on_left.wait_recv()

    def finish(self):
        for copy in (self.right, self.left, self.on_right, self.on_left):
            copy.wait_send()


class Direct:
    def __init__(self, block, place, p, sems, first):
        b = block(p)
        self.copies = [rcopy(b, b, sems, first + d - 1, place(up(p, d))) for d in (1, 2, 3)]

    def start(self):
        for copy in self.copies:
            copy.start()

    def arrive(self):
        for copy in self.copies:
            copy.wait_recv()

    def finish(self):
        for copy in self.copies:
            copy.wait_send()


def nt(a, b):
    return lax.dot_general(a, b, (((1,), (1,)), ((), ())), preferred_element_type=jnp.float32)


def tn(a, b):
    return lax.dot_general(a, b, (((0,), (0,)), ((), ())), preferred_element_type=jnp.float32)


def nn(a, b):
    return jnp.dot(a, b, preferred_element_type=jnp.float32)


FACTOR = 128 ** (-0.5)
BF = jnp.bfloat16
F32 = jnp.float32


def add(out, terms):
    @pl.loop(0, out.shape[0])
    def _(i):
        value = terms[0][i].astype(F32)
        for term in terms[1:]:
            value = value + term[i].astype(F32)
        out[i] = value.astype(out.dtype)


class DirectSum:
    def __init__(self, part, place, p, sems, first, land, total):
        self.own, self.land, self.total = part(p), land, total
        self.copies = [rcopy(part(up(p, d)), land.at[d - 1], sems, first + d - 1, place(up(p, d))) for d in (1, 2, 3)]

    def start(self):
        for copy in self.copies:
            copy.start()

    def finish(self):
        for copy in self.copies:
            copy.wait_recv()
        add(self.total, [self.own] + [self.land.at[d] for d in range(3)])

    def drain(self):
        for copy in self.copies:
            copy.wait_send()


class RingSum:
    def __init__(self, part, place, p, sems, first, via, land, total):
        self.part, self.place, self.p, self.sems, self.first = part, place, p, sems, first
        self.via, self.land, self.total = via, land, total

    def copy(self, i, src, dst, step):
        c = rcopy(src, dst, self.sems, self.first + i, self.place(up(self.p, step)))
        c.start()
        return c

    def start(self):
        p = self.p
        self.a = self.copy(0, self.part(up(p, 2), 0), self.via.at[0], 1)
        self.b = self.copy(1, self.part(up(p, 2), 1), self.via.at[1], 3)
        self.d = self.copy(2, self.part(up(p, 1), 1), self.land.at[0, 1], 1)
        self.e = self.copy(3, self.part(up(p, 3), 0), self.land.at[1, 0], 3)

    def relay(self):
        p = self.p
        self.a.wait_recv()
        add(self.via.at[2], [self.via.at[0], self.part(up(p, 1), 0)])
        self.f = self.copy(4, self.via.at[2], self.land.at[0, 0], 1)
        self.b.wait_recv()
        add(self.via.at[3], [self.via.at[1], self.part(up(p, 3), 1)])
        self.g = self.copy(5, self.via.at[3], self.land.at[1, 1], 3)

    def finish(self):
        for c in (self.d, self.e, self.f, self.g):
            c.wait_recv()
        for h in range(2):
            add(self.total(h), [self.part(self.p, h), self.land.at[0, h], self.land.at[1, h]])

    def drain(self):
        for c in (self.a, self.b, self.d, self.e, self.f, self.g):
            c.wait_send()


def wait_bytes(ref, sem):
    pltpu.make_async_copy(ref, ref, sem).wait()


def block_kernel(tok, cot, wq, wk, wv, w_out, gain_in, mixed, grad, g_q, g_k, g_v, g_o, gsum,
                 t, cth, w, wo, wom, normed, cotm, scaled, proj, ups, upt, back, atts, atth, attm, mask,
                 mrh, dp, dr, om, og, gh,
                 via1, land1, sum1, land2, sum2, land3, p3, p3r,
                 dvia, dland, d1, dland2, d2, dland3, evia, eland, e1, eland2, e2, eland3,
                 fvia, fland, f1, fland2, f2, fland3, q3,
                 gain, gg, gland, gacc,
                 ag_s, ag_r, w_s, w_r, w_l, in_s, in_r, fw_s, fw_r, c_s, c_r, up_s, up_r, at_s, at_r, sw_s, sw_r,
                 bk_s, bk_r, rs_s, rs_r, gn_s, gn_r, loc, out_l):
    y, c, z, x = coords()
    tm = z * 4 + x
    sib = device(y, 1 - c, z, x)
    at_x = lambda v: device(y, c, z, v)
    at_y = lambda v: device(v, c, z, x)
    at_z = lambda v: device(y, c, v, x)
    mph = cth

    stage, cot_own = [], []
    for g in range(3):
        copy = pltpu.make_async_copy(tok.at[:, g], om.at[g], loc.at[g])
        copy.start()
        stage.append(copy)
    own_o = pltpu.make_async_copy(w_out, wo.at[y, z, x], loc.at[6])
    own_o.start()
    own_w = []
    for i, src in enumerate((wq, wk, wv)):
        for j in range(4):
            cols = pl.ds(pl.multiple_of((2 * j + c) * 128, 128), 128)
            copy = pltpu.make_async_copy(src.at[:, cols], w.at[i, y, c, z, x, :, pl.ds(128 * j, 128)], w_l.at[4 * i + j])
            copy.start()
            own_w.append(copy)
    for g in range(3):
        copy = pltpu.make_async_copy(cot.at[:, g], cth.at[g, c], loc.at[3 + g])
        copy.start()
        cot_own.append(copy)
    greet(y, c, z, x)

    swap_w = []
    for i, src in enumerate((wq, wk, wv)):
        for j in range(4):
            cols = pl.ds(pl.multiple_of((2 * j + 1 - c) * 128, 128), 128)
            copy = rcopy(src.at[:, cols], w.at[i, y, c, z, x, :, pl.ds(128 * j, 128)], (w_s, w_r), 4 * i + j, sib)
            copy.start()
            swap_w.append(copy)
    swap_c = []
    for g in range(3):
        cot_own[g].wait()
        copy = rcopy(cth.at[g, c], cth.at[g, c], (c_s, c_r), g, sib)
        copy.start()
        swap_c.append(copy)

    ag = (ag_s, ag_r)
    qa = Direct(lambda v: w.at[0, y, :, z, v], at_x, x, ag, 0)
    qb = Direct(lambda v: w.at[0, y, :, v], at_z, z, ag, 3)
    qc = Ring(lambda v: w.at[0, v], lambda v, k: w.at[0, v, k], at_y, y, ag, 6)
    ka = Direct(lambda v: w.at[1, y, :, v, x], at_z, z, ag, 10)
    kb = Direct(lambda v: w.at[1, v, :, :, x], at_y, y, ag, 13)
    kc = Ring(lambda v: w.at[1, :, :, :, v], lambda v, k: w.at[1, :, k, :, v], at_x, x, ag, 16)
    va = Direct(lambda v: w.at[2, v, :, z, x], at_y, y, ag, 20)
    vb = Direct(lambda v: w.at[2, :, :, z, v], at_x, x, ag, 23)
    vc = Ring(lambda v: w.at[2, :, :, v], lambda v, k: w.at[2, :, k, v], at_z, z, ag, 26)
    o0, o1, o2 = (pl.ds(0, CUT), pl.ds(CUT, (2048 - CUT) // 2), pl.ds(CUT + (2048 - CUT) // 2, (2048 - CUT) // 2))
    da = Direct(lambda v: wo.at[y, v, x, :, o0], at_z, z, ag, 30)
    db = Direct(lambda v: wo.at[y, :, v, :, o0], at_x, x, ag, 33)
    dc = Ring(lambda v: wo.at[v, :, :, :, o0], lambda v, k: wo.at[v, pl.ds(2 * k, 2), :, :, o0], at_y, y, ag, 36)
    ea = Direct(lambda v: wo.at[v, z, x, :, o1], at_y, y, ag, 40)
    eb = Direct(lambda v: wo.at[:, v, x, :, o1], at_z, z, ag, 43)
    ec = Ring(lambda v: wo.at[:, :, v, :, o1], lambda v, k: wo.at[pl.ds(2 * k, 2), :, v, :, o1], at_x, x, ag, 46)
    fa = Direct(lambda v: wo.at[y, z, v, :, o2], at_x, x, ag, 50)
    fb = Direct(lambda v: wo.at[v, z, :, :, o2], at_y, y, ag, 53)
    fc = Ring(lambda v: wo.at[:, v, :, :, o2], lambda v, k: wo.at[pl.ds(2 * k, 2), v, :, :, o2], at_z, z, ag, 56)
    firsts, seconds, thirds = (qa, ka, va, da, ea, fa), (qb, kb, vb, db, eb, fb), (qc, kc, vc, dc, ec, fc)
    rings = firsts + seconds + thirds

    def to_all(send):
        for dz, dx in OFFSETS:
            zz, xx = up(z, dz), up(x, dx)
            send(zz * 4 + xx, device(y, c, zz, xx))

    def spread(g):
        stage[g].wait()
        pltpu.make_async_copy(tok.at[tm, g], t.at[c, g, tm], in_r.at[g]).start()
        to_all(lambda j, place: rcopy(om.at[g, j], t.at[c, g, tm], (in_s, in_r), g, place).start())

    passed = {}

    def pass_on(g):
        wait_bytes(t.at[c, g], in_r.at[g])
        passed[g] = rcopy(t.at[c, g], t.at[c, g], (fw_s, fw_r), g, sib)
        passed[g].start()

    def cot_rows():
        for g in range(3):
            swap_c[g].wait_recv()

            @pl.loop(0, 8)
            def _(i):
                k, f = lax.div(i, 4), lax.rem(i, 4) * 4
                rows = pl.ds(pl.multiple_of(g * 256 + i * 32, 32), 32)
                cotm[rows, :] = cth[g, k, pl.ds(f, 4)].astype(F32).reshape(32, 2048).astype(BF)

    def wo_rows():
        @pl.loop(0, 4)
        def _(j):
            wom[pl.ds(pl.multiple_of(j * 128, 128), 128), :] = wo[j].astype(F32).reshape(128, 2048).astype(BF)

    def upstream():
        @pl.loop(0, 3)
        def _(g):
            rows = pl.ds(pl.multiple_of(g * 256, 256), 256)
            ups[g] = nt(cotm[rows, :], wom[...]).reshape(2, 16, 8, 512).astype(BF)

        pltpu.make_async_copy(ups.at[:, :, tm], upt.at[:, :, tm], up_r.at[0]).start()
        to_all(lambda j, place: rcopy(ups.at[:, :, j], upt.at[:, :, tm], (up_s, up_r), 0, place).start())

    def norm(g):
        passed[g].wait_recv()

        @pl.loop(0, 8)
        def _(i):
            k, f = lax.div(i, 4), lax.rem(i, 4) * 4
            value = t[k, g, pl.ds(f, 4)].astype(F32).reshape(32, 2048)
            centered = value - jnp.mean(value, axis=-1, keepdims=True)
            inverse = lax.rsqrt(jnp.mean(centered * centered, axis=-1, keepdims=True) + 1e-05)
            s = centered * inverse
            scaled[pl.ds(pl.multiple_of(i * 32, 32), 32), :] = s
            rows = pl.ds(pl.multiple_of(g * 256 + i * 32, 32), 32)
            normed[rows, :] = (s * gain[...]).astype(BF)

    def project(g, i):
        rows = pl.ds(g * 256, 256)
        if i < 3:
            proj[i] = nn(normed[rows, :], w[i].reshape(2048, 512)).astype(BF)
        else:
            proj[3] = upt[g].astype(F32).reshape(256, 512).astype(BF)

    def attention(g):
        @pl.loop(0, 4)
        def _(h):
            cols = pl.ds(pl.multiple_of(h * 128, 128), 128)
            for clip in range(2):
                rows = pl.ds(clip * 128, 128)
                out = pl.ds(g * 256 + clip * 128, 128)
                q, k, v, u = (proj[j, rows, cols] for j in range(4))
                s = nt(q, k) * FACTOR + mask[...]
                e = jnp.exp(s - jnp.max(s, axis=-1, keepdims=True))
                p = e / jnp.sum(e, axis=-1, keepdims=True)
                p_b = p.astype(BF)
                atts[g, clip, :, :, cols] = nn(p_b, v).reshape(16, 8, 128).astype(BF)
                d = nt(u, v)
                ds = (p * (d - jnp.sum(p * d, axis=-1, keepdims=True))).astype(BF)
                back[0, out, cols] = (nn(ds, k) * FACTOR).astype(BF)
                back[1, out, cols] = (tn(ds, q) * FACTOR).astype(BF)
                back[2, out, cols] = tn(p_b, u).astype(BF)

        pltpu.make_async_copy(atts.at[g, :, tm], atth.at[g, :, tm], at_r.at[g]).start()
        to_all(lambda f, place: rcopy(atts.at[g, :, f], atth.at[g, :, tm], (at_s, at_r), g, place).start())

    swapped = {}

    def partials(g):
        rows = pl.ds(g * 256, 256)
        for h in range(2):
            half = pl.ds(h * 1024, 1024)
            dn = None
            for i in range(3):
                term = nt(back[i, rows, :], w[i, pl.ds(2 * h, 2)].reshape(1024, 512))
                dn = term if dn is None else dn + term
            dp[g, :, :, :, half] = dn.reshape(2, 16, 8, 1024).astype(BF)
            total = jnp.sum(dn * scaled[:, half], axis=0, keepdims=True)
            gg[:, half] = total if g == 0 else gg[:, half] + total
        swapped[g] = rcopy(dp.at[g, 1 - c], dr.at[g], (sw_s, sw_r), g, sib)
        swapped[g].start()

    def finalize(g):
        swapped[g].wait_recv()

        @pl.loop(0, 4)
        def _(i):
            fs = pl.ds(i * 4, 4)
            value = t[c, g, fs].astype(F32)
            centered = value - jnp.mean(value, axis=-1, keepdims=True)
            inverse = lax.rsqrt(jnp.mean(centered * centered, axis=-1, keepdims=True) + 1e-05)
            s = centered * inverse
            ds = (dp[g, c, fs].astype(F32) + dr[g, fs].astype(F32)) * gain[...].reshape(1, 1, 2048)
            first = jnp.mean(ds, axis=-1, keepdims=True)
            second = jnp.mean(ds * s, axis=-1, keepdims=True)
            og[g, fs] = (inverse * (ds - first - s * second)).astype(BF)

        pltpu.make_async_copy(og.at[g, tm], gh.at[g, tm], bk_r.at[g]).start()
        to_all(lambda f, place: rcopy(og.at[g, f], gh.at[g, tm], (bk_s, bk_r), g, place).start())

    mixed_swap, written = {}, []

    def home_rows(g):
        wait_bytes(atth.at[g], at_r.at[g])
        attm[pl.ds(g * 256, 256), :] = atth[g].astype(F32).reshape(256, 512).astype(BF)

    def home(g):
        rows = pl.ds(g * 256, 256)
        for h in range(2):
            half = pl.ds(h * 1024, 1024)
            mph[g, :, :, :, half] = nn(attm[rows, :], wom[:, half]).reshape(2, 16, 8, 1024).astype(BF)
        mixed_swap[g] = rcopy(mph.at[g, 1 - c], mrh.at[g], (sw_s, sw_r), 3 + g, sib)
        mixed_swap[g].start()

    def write(g, j, src, dst):
        copy = pltpu.make_async_copy(src.at[g], dst.at[:, g], out_l.at[2 * g + j])
        copy.start()
        written.append(copy)

    def mixed_out(g):
        wait_bytes(om.at[g, pl.ds(0, 15)], in_s.at[g])
        mixed_swap[g].wait_recv()

        @pl.loop(0, 4)
        def _(i):
            js = pl.ds(i * 4, 4)
            om[g, js] = (om[g, js].astype(F32) + (mph[g, c, js].astype(F32) + mrh[g, js].astype(F32))).astype(BF)

        write(g, 0, om, mixed)

    def grad_out(g):
        wait_bytes(gh.at[g], bk_r.at[g])

        @pl.loop(0, 4)
        def _(i):
            js = pl.ds(i * 4, 4)
            rows = pl.ds(pl.multiple_of(g * 256 + c * 128 + i * 32, 32), 32)
            gh[g, js] = (gh[g, js].astype(F32) + cotm[rows, :].astype(F32).reshape(4, 8, 2048)).astype(BF)

        write(g, 1, gh, grad)

    def w_terms(i):
        @pl.loop(0, 8)
        def _(b):
            cols = pl.ds(pl.multiple_of(b * 256, 256), 256)
            w[i, lax.div(b, 2), lax.rem(b, 2)] = tn(normed[:, cols], back[i]).reshape(4, 4, 16, 512).astype(BF)

    def o_terms():
        @pl.loop(0, 2)
        def _(b):
            cols = pl.ds(pl.multiple_of(b * 256, 256), 256)
            wo[pl.ds(2 * b, 2)] = tn(attm[:, cols], cotm[...]).reshape(2, 4, 4, 8, 2048).astype(BF)

    rs = (rs_s, rs_r)

    def term_ring(i, part, place, p):
        return RingSum(part, place, p, rs, 12 * i, via1.at[i], land1.at[i], lambda h: sum1.at[i, h])

    def term_sums(i, part2, place2, p2, place3, p3_):
        second = DirectSum(part2, place2, p2, rs, 12 * i + 6, land2.at[i], sum2.at[i])
        third = DirectSum(lambda v: sum2.at[i, :, v], place3, p3_, rs, 12 * i + 9, land3.at[i], p3.at[i])
        return second, third

    qx = term_ring(0, lambda v, h: w.at[0, v, h], at_y, y)
    qy, qz = term_sums(0, lambda v: sum1.at[0, :, v], at_z, z, at_x, x)
    kx = term_ring(1, lambda v, h: w.at[1, :, h, :, v], at_x, x)
    ky, kz = term_sums(1, lambda v: sum1.at[1, :, v], at_y, y, at_z, z)
    vx = term_ring(2, lambda v, h: w.at[2, :, h, v], at_z, z)
    vy, vz = term_sums(2, lambda v: sum1.at[2, :, :, v], at_x, x, at_y, y)
    dx = RingSum(lambda v, h: wo.at[v, pl.ds(2 * h, 2), :, :, o0], at_y, y, rs, 36, dvia, dland, lambda h: d1.at[pl.ds(2 * h, 2)])
    dy = DirectSum(lambda v: d1.at[:, v], at_x, x, rs, 42, dland2, d2)
    dz = DirectSum(lambda v: d2.at[pl.ds(v, 1)], at_z, z, rs, 45, dland3, q3.at[:, :, o0])
    ex = RingSum(lambda v, h: wo.at[pl.ds(2 * h, 2), :, v, :, o1], at_x, x, rs, 48, evia, eland, lambda h: e1.at[pl.ds(2 * h, 2)])
    ey = DirectSum(lambda v: e1.at[:, v], at_z, z, rs, 54, eland2, e2)
    ez = DirectSum(lambda v: e2.at[pl.ds(v, 1)], at_y, y, rs, 57, eland3, q3.at[:, :, o1])
    fx = RingSum(lambda v, h: wo.at[pl.ds(2 * h, 2), v, :, :, o2], at_z, z, rs, 60, fvia, fland, lambda h: f1.at[pl.ds(2 * h, 2)])
    fy = DirectSum(lambda v: f1.at[v], at_y, y, rs, 66, fland2, f2)
    fz = DirectSum(lambda v: f2.at[pl.ds(v, 1)], at_x, x, rs, 69, fland3, q3.at[:, :, o2])
    all_sums = (qx, qy, qz, kx, ky, kz, vx, vy, vz, dx, dy, dz, ex, ey, ez, fx, fy, fz)

    def gain_start(k, src):
        place, p = [(at_y, y), (at_z, z), (at_x, x)][k]
        out = []
        for d in (1, 2, 3):
            copy = rcopy(src, gland.at[3 * k + d - 1], (gn_s, gn_r), 3 * k + d - 1, place(up(p, d)))
            copy.start()
            out.append(copy)
        return out

    def gain_finish(k, src, copies):
        for copy in copies:
            copy.wait_recv()
        gacc[k] = src[...] + gland[3 * k] + gland[3 * k + 1] + gland[3 * k + 2]

    own_o.wait()
    for r in (da, ea, fa):
        r.start()
    for copy in own_w:
        copy.wait()
    for copy in swap_w:
        copy.wait_recv()
    for r in (qa, ka, va):
        r.start()
    gain[...] = gain_in[...].astype(F32).reshape(1, 2048)
    rows_i = lax.broadcasted_iota(jnp.int32, (128, 128), 0)
    cols_i = lax.broadcasted_iota(jnp.int32, (128, 128), 1)
    same = lax.rem(rows_i + 128 - cols_i, 8) == 0
    mask[...] = jnp.where(same & (cols_i <= rows_i), 0.0, -1e30)
    for a, b in ((da, db), (ea, eb), (fa, fb), (qa, qb), (ka, kb), (va, vb)):
        a.arrive()
        b.start()
    for a, b in ((db, dc), (eb, ec), (fb, fc), (qb, qc), (kb, kc), (vb, vc)):
        a.arrive()
        b.start()
    spread(0)
    cot_rows()
    for r in (dc, ec, fc):
        r.relay()
    for r in (qc, kc, vc):
        r.relay()
    for r in (dc, ec, fc):
        r.arrive()
    wo_rows()
    upstream()
    spread(1)
    pass_on(0)
    norm(0)
    qc.arrive()
    project(0, 0)
    vc.arrive()
    project(0, 2)
    kc.arrive()
    project(0, 1)
    spread(2)
    wait_bytes(upt, up_r.at[0])
    project(0, 3)
    attention(0)
    partials(0)
    pass_on(1)
    norm(1)
    for i in range(4):
        project(1, i)
    pass_on(2)
    finalize(0)
    attention(1)
    partials(1)
    norm(2)
    for i in range(4):
        project(2, i)
    finalize(1)
    attention(2)
    for r in rings:
        r.finish()
    for copy in swap_c:
        copy.wait_send()
    partials(2)
    w_terms(0)
    qx.start()
    home_rows(0)
    home_rows(1)
    w_terms(1)
    kx.start()
    home_rows(2)
    o_terms()
    for r in (dx, ex, fx):
        r.start()
    w_terms(2)
    vx.start()
    finalize(2)
    qx.relay()
    kx.relay()
    for r in (dx, ex, fx):
        r.relay()
    home(0)
    vx.relay()
    for i in range(16):
        gland[9, pl.ds(i, 1), :] = gg[:, pl.ds(128 * i, 128)]
    g0 = gain_start(0, gland.at[9])
    home(1)
    home(2)
    for a, b in ((qx, qy), (kx, ky), (dx, dy), (ex, ey), (fx, fy)):
        a.finish()
        b.start()
    gain_finish(0, gland.at[9], g0)
    g1 = gain_start(1, gacc.at[0])
    vx.finish()
    vy.start()
    mixed_out(0)
    mixed_out(1)
    mixed_out(2)
    grad_out(0)
    grad_out(1)
    for a, b in ((qy, qz), (ky, kz), (dy, dz), (ey, ez), (fy, fz)):
        a.finish()
        b.start()
    gain_finish(1, gacc.at[0], g1)
    g2 = gain_start(2, gacc.at[1])
    vy.finish()
    vz.start()
    grad_out(2)
    gain_finish(2, gacc.at[1], g2)
    g3 = rcopy(gacc.at[2], gland.at[10], (gn_s, gn_r), 9, sib)
    g3.start()
    last = {}

    def across(i):
        copy = rcopy(p3.at[i, 1 - c], p3r.at[i], (sw_s, sw_r), 6 + i, sib)
        copy.start()
        last[i] = copy

    def put(i, out):
        last[i].wait_recv()
        for j in range(4):
            cols = pl.ds(128 * j, 128)
            out[:, pl.ds(pl.multiple_of((2 * j + c) * 128, 128), 128)] = p3[i, c, :, cols]
            out[:, pl.ds(pl.multiple_of((2 * j + 1 - c) * 128, 128), 128)] = p3r[i, :, cols]

    for r in (dz, ez, fz):
        r.finish()
    for i, r in enumerate((qz, kz, vz)):
        r.finish()
        across(i)
    g_o[...] = q3[0]
    g3.wait_recv()
    gsum[...] = gacc[2] + gland[10]
    put(0, g_q)
    put(1, g_k)
    put(2, g_v)
    wait_bytes(ups.at[:, :, pl.ds(0, 15)], up_s.at[0])
    for g in range(3):
        wait_bytes(atts.at[g, :, pl.ds(0, 15)], at_s.at[g])
        wait_bytes(og.at[g, pl.ds(0, 15)], bk_s.at[g])
    for copy in written:
        copy.wait()
    for copies in (swap_w, passed.values(), swapped.values(), mixed_swap.values(), g0, g1, g2, [g3], last.values()):
        for copy in copies:
            copy.wait_send()
    for r in all_sums:
        r.drain()


def block_call(tok, cot, wq, wk, wv, w_out, gain):
    vm = pl.BlockSpec(memory_space=pltpu.VMEM)
    any_ = pl.BlockSpec(memory_space=pl.ANY)
    sds = jax.ShapeDtypeStruct
    V = pltpu.VMEM
    sem = pltpu.SemaphoreType.DMA
    rows = (16, 3, 8, 2048)
    groups = (3, 16, 8, 2048)

    def ring(lead, unit):
        return [V(lead + (4,) + unit, BF), V(lead + (2, 2) + unit, BF)]

    def out_sums(n):
        return ring((), (2, 4, 8, n)) + [V(u, BF) for u in ((4, 4, 8, n), (3, 4, 8, n), (4, 8, n), (3, 1, 8, n))]

    sems = [60, 60, 12, 12, 12, 3, 3, 3, 3, 3, 3, 1, 1, 3, 3, 9, 9, 3, 3, 72, 72, 10, 10, 7, 6]
    return pl.pallas_call(
        block_kernel,
        out_shape=(sds(rows, BF), sds(rows, BF))
        + (sds((16, 1024), F32),) * 3
        + (sds((8, 2048), F32), sds((16, 128), F32)),
        in_specs=[any_] * 6 + [vm],
        out_specs=(any_, any_) + (vm,) * 5,
        scratch_shapes=[V((2, 3, 16, 8, 2048), BF), V((3, 2, 16, 8, 2048), BF)]
        + [V((3, 4, 2, 4, 4, 16, 512), BF), V((4, 4, 4, 8, 2048), BF), V((512, 2048), BF)]
        + [V((768, 2048), BF)] * 2
        + [V((256, 2048), F32), V((4, 256, 512), BF)]
        + [V((3, 2, 16, 8, 512), BF)] * 2
        + [V((3, 768, 512), BF)]
        + [V((3, 2, 16, 8, 512), BF)] * 2
        + [V((768, 512), BF), V((128, 128), F32)]
        + [V(groups, BF), V((3, 2, 16, 8, 2048), BF)]
        + [V(groups, BF)] * 4
        + ring((3,), (4, 4, 16, 512))
        + [V((3, 2, 4, 4, 16, 512), BF)]
        + [V((3, 3, 2, 4, 16, 512), BF)]
        + [V((3, 2, 4, 16, 512), BF)]
        + [V((3, 3, 2, 16, 512), BF)]
        + [V((3, 2, 16, 512), F32), V((3, 16, 512), F32)]
        + out_sums(CUT)
        + out_sums((2048 - CUT) // 2)
        + out_sums((2048 - CUT) // 2)
        + [V((1, 8, 2048), F32)]
        + [V((1, 2048), F32), V((1, 2048), F32), V((11, 16, 128), F32), V((3, 16, 128), F32)]
        + [sem((n,)) for n in sems],
        compiler_params=pltpu.CompilerParams(collective_id=0, has_side_effects=True, vmem_limit_bytes=VMEM_LIMIT),
        name="block",
    )(tok, cot, wq, wk, wv, w_out, gain)


def finish_kernel(*refs):
    ins, outs, gsum, gain_out, held, sems = refs[:6], refs[7:13], refs[6], refs[13], refs[14:20], refs[20]
    pieces = [(i, pl.ds(4 * k, 4)) for i in range(2) for k in range(4)] + [(i, slice(None)) for i in range(2, 6)]
    enter = [pltpu.make_async_copy(ins[i].at[at], held[i].at[at], sems.at[n]) for n, (i, at) in enumerate(pieces)]
    leave = [pltpu.make_async_copy(held[i].at[at], outs[i].at[at], sems.at[12 + n]) for n, (i, at) in enumerate(pieces)]
    for copy in enter:
        copy.start()
    index = lax.axis_index("dp") * 16 + lax.axis_index("tm")
    row = gsum[pl.ds(lax.div(index, 8), 1), :]
    out = jnp.zeros((1, 16), F32)
    for i in range(8):
        out = jnp.where(lax.rem(index, 8) == i, row[:, 16 * i : 16 * i + 16], out)
    gain_out[...] = out
    for before, after in zip(enter, leave):
        before.wait()
        after.start()
    for copy in leave:
        copy.wait()


def finish_call(arrays, gsum):
    vm = pl.BlockSpec(memory_space=pltpu.VMEM)
    any_ = pl.BlockSpec(memory_space=pl.ANY)
    return pl.pallas_call(
        finish_kernel,
        out_shape=tuple(jax.ShapeDtypeStruct(a.shape, a.dtype) for a in arrays) + (jax.ShapeDtypeStruct((1, 16), F32),),
        in_specs=[any_] * 6 + [vm],
        out_specs=(any_,) * 6 + (vm,),
        scratch_shapes=[pltpu.VMEM(a.shape, a.dtype) for a in arrays] + [pltpu.SemaphoreType.DMA((24,))],
        name="finish",
    )(*arrays, gsum)


def on_device(tokens, cotangent, norm_gain, w_query, w_key, w_value, w_out):
    tok = tokens.reshape(16, 3, 8, 2048)
    cot = cotangent.reshape(16, 3, 8, 2048)
    gain = norm_gain
    *arrays, gsum = block_call(tok, cot, w_query, w_key, w_value, w_out, gain)
    mixed, grad, g_q, g_k, g_v, g_o, grad_gain = finish_call(arrays, gsum)
    shape = (1, 1, 384, 2048)
    return mixed.reshape(shape), grad.reshape(shape), grad_gain.reshape(16), g_q, g_k, g_v, g_o


def solution(mesh):
    rows = P("dp", "tm", None, None)
    weight = P(("dp", "tm"), None)
    return jax.shard_map(
        on_device,
        mesh=mesh,
        in_specs=(rows, rows, P()) + (weight,) * 4,
        out_specs=(rows, rows, P(("dp", "tm"))) + (weight,) * 4,
        check_vma=False,
    )
```

```python
import functools

import jax
import jax.numpy as jnp
from jax import lax
from jax.experimental import pallas as pl
from jax.experimental.pallas import tpu as pltpu
from jax.sharding import PartitionSpec as P

MESH = pl.DeviceIdType.MESH
CUT = 768
VMEM_LIMIT = 62 * 1024 * 1024


def coords():
    dp, tm = lax.axis_index("dp"), lax.axis_index("tm")
    return lax.div(dp, 2), lax.rem(dp, 2), lax.div(tm, 4), lax.rem(tm, 4)


def device(y, c, z, x):
    return {"dp": y * 2 + c, "tm": z * 4 + x}


def up(p, d):
    return lax.rem(p + d, 4)


def rcopy(src, dst, sems, i, where):
    return pltpu.make_async_remote_copy(
        src_ref=src,
        dst_ref=dst,
        send_sem=sems[0].at[i],
        recv_sem=sems[1].at[i],
        device_id=where,
        device_id_type=MESH,
    )


OFFSETS = [
    (0, 1), (0, 3), (1, 0), (3, 0), (1, 1), (3, 3), (1, 3), (3, 1),
    (2, 2), (0, 2), (2, 0), (2, 1), (2, 3), (1, 2), (3, 2),
]


def greet(y, c, z, x, tm_peers=True):
    barrier = pltpu.get_barrier_semaphore()
    peers = [device(y, 1 - c, z, x)] + [device(up(y, d), c, z, x) for d in (1, 2, 3)]
    peers += [device(y, c, up(z, dz), up(x, dx)) for dz, dx in OFFSETS]
    for peer in peers:
        pl.semaphore_signal(barrier, inc=1, device_id=peer, device_id_type=MESH)
    pl.semaphore_wait(barrier, len(peers))


class Ring:
    def __init__(self, block, half, place, p, sems, first):
        self.block, self.half, self.place, self.p = block, half, place, p
        self.sems, self.first = sems, first

    def start(self):
        p, b = self.p, self.block(self.p)
        self.right = rcopy(b, b, self.sems, self.first, self.place(up(p, 1)))
        self.left = rcopy(b, b, self.sems, self.first + 1, self.place(up(p, 3)))
        self.right.start()
        self.left.start()

    def relay(self):
        p = self.p
        self.right.wait_recv()
        h = self.half(up(p, 3), 0)
        self.on_right = rcopy(h, h, self.sems, self.first + 2, self.place(up(p, 1)))
        self.on_right.start()
        self.left.wait_recv()
        h = self.half(up(p, 1), 1)
        self.on_left = rcopy(h, h, self.sems, self.first + 3, self.place(up(p, 3)))
        self.on_left.start()

    def arrive(self):
        self.on_right.wait_recv()
        self.on_left.wait_recv()

    def finish(self):
        for copy in (self.right, self.left, self.on_right, self.on_left):
            copy.wait_send()


class Direct:
    def __init__(self, block, place, p, sems, first):
        b = block(p)
        self.copies = [rcopy(b, b, sems, first + d - 1, place(up(p, d))) for d in (1, 2, 3)]

    def start(self):
        for copy in self.copies:
            copy.start()

    def arrive(self):
        for copy in self.copies:
            copy.wait_recv()

    def finish(self):
        for copy in self.copies:
            copy.wait_send()


def nt(a, b):
    return lax.dot_general(a, b, (((1,), (1,)), ((), ())), preferred_element_type=jnp.float32)


def tn(a, b):
    return lax.dot_general(a, b, (((0,), (0,)), ((), ())), preferred_element_type=jnp.float32)


def nn(a, b):
    return jnp.dot(a, b, preferred_element_type=jnp.float32)


FACTOR = 128 ** (-0.5)
BF = jnp.bfloat16
F32 = jnp.float32


def add(out, terms):
    @pl.loop(0, out.shape[0])
    def _(i):
        value = terms[0][i].astype(F32)
        for term in terms[1:]:
            value = value + term[i].astype(F32)
        out[i] = value.astype(out.dtype)


class DirectSum:
    def __init__(self, part, place, p, sems, first, land, total):
        self.own, self.land, self.total = part(p), land, total
        self.copies = [rcopy(part(up(p, d)), land.at[d - 1], sems, first + d - 1, place(up(p, d))) for d in (1, 2, 3)]

    def start(self):
        for copy in self.copies:
            copy.start()

    def finish(self):
        for copy in self.copies:
            copy.wait_recv()
        add(self.total, [self.own] + [self.land.at[d] for d in range(3)])

    def drain(self):
        for copy in self.copies:
            copy.wait_send()


class RingSum:
    def __init__(self, part, place, p, sems, first, via, land, total):
        self.part, self.place, self.p, self.sems, self.first = part, place, p, sems, first
        self.via, self.land, self.total = via, land, total

    def copy(self, i, src, dst, step):
        c = rcopy(src, dst, self.sems, self.first + i, self.place(up(self.p, step)))
        c.start()
        return c

    def start(self):
        p = self.p
        self.a = self.copy(0, self.part(up(p, 2), 0), self.via.at[0], 1)
        self.b = self.copy(1, self.part(up(p, 2), 1), self.via.at[1], 3)
        self.d = self.copy(2, self.part(up(p, 1), 1), self.land.at[0, 1], 1)
        self.e = self.copy(3, self.part(up(p, 3), 0), self.land.at[1, 0], 3)

    def relay(self):
        p = self.p
        self.a.wait_recv()
        add(self.via.at[2], [self.via.at[0], self.part(up(p, 1), 0)])
        self.f = self.copy(4, self.via.at[2], self.land.at[0, 0], 1)
        self.b.wait_recv()
        add(self.via.at[3], [self.via.at[1], self.part(up(p, 3), 1)])
        self.g = self.copy(5, self.via.at[3], self.land.at[1, 1], 3)

    def finish(self):
        for c in (self.d, self.e, self.f, self.g):
            c.wait_recv()
        for h in range(2):
            add(self.total(h), [self.part(self.p, h), self.land.at[0, h], self.land.at[1, h]])

    def drain(self):
        for c in (self.a, self.b, self.d, self.e, self.f, self.g):
            c.wait_send()


def wait_bytes(ref, sem):
    pltpu.make_async_copy(ref, ref, sem).wait()


def block_kernel(tok, cot, wq, wk, wv, w_out, gain_in, mixed, grad, g_q, g_k, g_v, g_o, gsum,
                 t, cth, w, wo, wom, normed, cotm, scaled, proj, ups, upt, back, atts, atth, attm, mask,
                 mrh, dp, dr, om, og, gh,
                 via1, land1, sum1, land2, sum2, land3, p3, p3r,
                 dvia, dland, d1, dland2, d2, dland3, evia, eland, e1, eland2, e2, eland3,
                 fvia, fland, f1, fland2, f2, fland3, q3,
                 gain, gg, gland, gacc,
                 ag_s, ag_r, w_s, w_r, w_l, in_s, in_r, fw_s, fw_r, c_s, c_r, up_s, up_r, at_s, at_r, sw_s, sw_r,
                 bk_s, bk_r, rs_s, rs_r, gn_s, gn_r, loc, out_l):
    y, c, z, x = coords()
    tm = z * 4 + x
    sib = device(y, 1 - c, z, x)
    at_x = lambda v: device(y, c, z, v)
    at_y = lambda v: device(v, c, z, x)
    at_z = lambda v: device(y, c, v, x)
    mph = cth

    stage, cot_own = [], []
    for g in range(3):
        copy = pltpu.make_async_copy(tok.at[:, g], om.at[g], loc.at[g])
        copy.start()
        stage.append(copy)
    own_o = pltpu.make_async_copy(w_out, wo.at[y, z, x], loc.at[6])
    own_o.start()
    own_w = []
    for i, src in enumerate((wq, wk, wv)):
        for j in range(4):
            cols = pl.ds(pl.multiple_of((2 * j + c) * 128, 128), 128)
            copy = pltpu.make_async_copy(src.at[:, cols], w.at[i, y, c, z, x, :, pl.ds(128 * j, 128)], w_l.at[4 * i + j])
            copy.start()
            own_w.append(copy)
    for g in range(3):
        copy = pltpu.make_async_copy(cot.at[:, g], cth.at[g, c], loc.at[3 + g])
        copy.start()
        cot_own.append(copy)
    greet(y, c, z, x)

    swap_w = []
    for i, src in enumerate((wq, wk, wv)):
        for j in range(4):
            cols = pl.ds(pl.multiple_of((2 * j + 1 - c) * 128, 128), 128)
            copy = rcopy(src.at[:, cols], w.at[i, y, c, z, x, :, pl.ds(128 * j, 128)], (w_s, w_r), 4 * i + j, sib)
            copy.start()
            swap_w.append(copy)
    swap_c = []
    for g in range(3):
        cot_own[g].wait()
        copy = rcopy(cth.at[g, c], cth.at[g, c], (c_s, c_r), g, sib)
        copy.start()
        swap_c.append(copy)

    ag = (ag_s, ag_r)
    qa = Direct(lambda v: w.at[0, y, :, z, v], at_x, x, ag, 0)
    qb = Direct(lambda v: w.at[0, y, :, v], at_z, z, ag, 3)
    qc = Ring(lambda v: w.at[0, v], lambda v, k: w.at[0, v, k], at_y, y, ag, 6)
    ka = Direct(lambda v: w.at[1, y, :, v, x], at_z, z, ag, 10)
    kb = Direct(lambda v: w.at[1, v, :, :, x], at_y, y, ag, 13)
    kc = Ring(lambda v: w.at[1, :, :, :, v], lambda v, k: w.at[1, :, k, :, v], at_x, x, ag, 16)
    va = Direct(lambda v: w.at[2, v, :, z, x], at_y, y, ag, 20)
    vb = Direct(lambda v: w.at[2, :, :, z, v], at_x, x, ag, 23)
    vc = Ring(lambda v: w.at[2, :, :, v], lambda v, k: w.at[2, :, k, v], at_z, z, ag, 26)
    o0, o1, o2 = (pl.ds(0, CUT), pl.ds(CUT, (2048 - CUT) // 2), pl.ds(CUT + (2048 - CUT) // 2, (2048 - CUT) // 2))
    da = Direct(lambda v: wo.at[y, v, x, :, o0], at_z, z, ag, 30)
    db = Direct(lambda v: wo.at[y, :, v, :, o0], at_x, x, ag, 33)
    dc = Ring(lambda v: wo.at[v, :, :, :, o0], lambda v, k: wo.at[v, pl.ds(2 * k, 2), :, :, o0], at_y, y, ag, 36)
    ea = Direct(lambda v: wo.at[v, z, x, :, o1], at_y, y, ag, 40)
    eb = Direct(lambda v: wo.at[:, v, x, :, o1], at_z, z, ag, 43)
    ec = Ring(lambda v: wo.at[:, :, v, :, o1], lambda v, k: wo.at[pl.ds(2 * k, 2), :, v, :, o1], at_x, x, ag, 46)
    fa = Direct(lambda v: wo.at[y, z, v, :, o2], at_x, x, ag, 50)
    fb = Direct(lambda v: wo.at[v, z, :, :, o2], at_y, y, ag, 53)
    fc = Ring(lambda v: wo.at[:, v, :, :, o2], lambda v, k: wo.at[pl.ds(2 * k, 2), v, :, :, o2], at_z, z, ag, 56)
    firsts, seconds, thirds = (qa, ka, va, da, ea, fa), (qb, kb, vb, db, eb, fb), (qc, kc, vc, dc, ec, fc)
    rings = firsts + seconds + thirds

    def to_all(send):
        for dz, dx in OFFSETS:
            zz, xx = up(z, dz), up(x, dx)
            send(zz * 4 + xx, device(y, c, zz, xx))

    def spread(g):
        stage[g].wait()
        pltpu.make_async_copy(tok.at[tm, g], t.at[c, g, tm], in_r.at[g]).start()
        to_all(lambda j, place: rcopy(om.at[g, j], t.at[c, g, tm], (in_s, in_r), g, place).start())

    passed = {}

    def pass_on(g):
        wait_bytes(t.at[c, g], in_r.at[g])
        passed[g] = rcopy(t.at[c, g], t.at[c, g], (fw_s, fw_r), g, sib)
        passed[g].start()

    def cot_rows():
        for g in range(3):
            swap_c[g].wait_recv()

            @pl.loop(0, 8)
            def _(i):
                k, f = lax.div(i, 4), lax.rem(i, 4) * 4
                rows = pl.ds(pl.multiple_of(g * 256 + i * 32, 32), 32)
                cotm[rows, :] = cth[g, k, pl.ds(f, 4)].astype(F32).reshape(32, 2048).astype(BF)

    def wo_rows():
        @pl.loop(0, 4)
        def _(j):
            wom[pl.ds(pl.multiple_of(j * 128, 128), 128), :] = wo[j].astype(F32).reshape(128, 2048).astype(BF)

    def upstream():
        @pl.loop(0, 3)
        def _(g):
            rows = pl.ds(pl.multiple_of(g * 256, 256), 256)
            ups[g] = nt(cotm[rows, :], wom[...]).reshape(2, 16, 8, 512).astype(BF)

        pltpu.make_async_copy(ups.at[:, :, tm], upt.at[:, :, tm], up_r.at[0]).start()
        to_all(lambda j, place: rcopy(ups.at[:, :, j], upt.at[:, :, tm], (up_s, up_r), 0, place).start())

    def norm(g):
        passed[g].wait_recv()

        @pl.loop(0, 8)
        def _(i):
            k, f = lax.div(i, 4), lax.rem(i, 4) * 4
            value = t[k, g, pl.ds(f, 4)].astype(F32).reshape(32, 2048)
            centered = value - jnp.mean(value, axis=-1, keepdims=True)
            inverse = lax.rsqrt(jnp.mean(centered * centered, axis=-1, keepdims=True) + 1e-05)
            s = centered * inverse
            scaled[pl.ds(pl.multiple_of(i * 32, 32), 32), :] = s
            rows = pl.ds(pl.multiple_of(g * 256 + i * 32, 32), 32)
            normed[rows, :] = (s * gain[...]).astype(BF)

    def project(g, i):
        rows = pl.ds(g * 256, 256)
        if i < 3:
            proj[i] = nn(normed[rows, :], w[i].reshape(2048, 512)).astype(BF)
        else:
            proj[3] = upt[g].astype(F32).reshape(256, 512).astype(BF)

    def attention(g):
        @pl.loop(0, 4)
        def _(h):
            cols = pl.ds(pl.multiple_of(h * 128, 128), 128)
            for clip in range(2):
                rows = pl.ds(clip * 128, 128)
                out = pl.ds(g * 256 + clip * 128, 128)
                q, k, v, u = (proj[j, rows, cols] for j in range(4))
                s = nt(q, k) * FACTOR + mask[...]
                e = jnp.exp(s - jnp.max(s, axis=-1, keepdims=True))
                p = e / jnp.sum(e, axis=-1, keepdims=True)
                p_b = p.astype(BF)
                atts[g, clip, :, :, cols] = nn(p_b, v).reshape(16, 8, 128).astype(BF)
                d = nt(u, v)
                ds = (p * (d - jnp.sum(p * d, axis=-1, keepdims=True))).astype(BF)
                back[0, out, cols] = (nn(ds, k) * FACTOR).astype(BF)
                back[1, out, cols] = (tn(ds, q) * FACTOR).astype(BF)
                back[2, out, cols] = tn(p_b, u).astype(BF)

        pltpu.make_async_copy(atts.at[g, :, tm], atth.at[g, :, tm], at_r.at[g]).start()
        to_all(lambda f, place: rcopy(atts.at[g, :, f], atth.at[g, :, tm], (at_s, at_r), g, place).start())

    swapped = {}

    def partials(g):
        rows = pl.ds(g * 256, 256)
        for h in range(2):
            half = pl.ds(h * 1024, 1024)
            dn = None
            for i in range(3):
                term = nt(back[i, rows, :], w[i, pl.ds(2 * h, 2)].reshape(1024, 512))
                dn = term if dn is None else dn + term
            dp[g, :, :, :, half] = dn.reshape(2, 16, 8, 1024).astype(BF)
            total = jnp.sum(dn * scaled[:, half], axis=0, keepdims=True)
            gg[:, half] = total if g == 0 else gg[:, half] + total
        swapped[g] = rcopy(dp.at[g, 1 - c], dr.at[g], (sw_s, sw_r), g, sib)
        swapped[g].start()

    def finalize(g):
        swapped[g].wait_recv()

        @pl.loop(0, 4)
        def _(i):
            fs = pl.ds(i * 4, 4)
            value = t[c, g, fs].astype(F32)
            centered = value - jnp.mean(value, axis=-1, keepdims=True)
            inverse = lax.rsqrt(jnp.mean(centered * centered, axis=-1, keepdims=True) + 1e-05)
            s = centered * inverse
            ds = (dp[g, c, fs].astype(F32) + dr[g, fs].astype(F32)) * gain[...].reshape(1, 1, 2048)
            first = jnp.mean(ds, axis=-1, keepdims=True)
            second = jnp.mean(ds * s, axis=-1, keepdims=True)
            og[g, fs] = (inverse * (ds - first - s * second)).astype(BF)

        pltpu.make_async_copy(og.at[g, tm], gh.at[g, tm], bk_r.at[g]).start()
        to_all(lambda f, place: rcopy(og.at[g, f], gh.at[g, tm], (bk_s, bk_r), g, place).start())

    mixed_swap, written = {}, []

    def home_rows(g):
        wait_bytes(atth.at[g], at_r.at[g])
        attm[pl.ds(g * 256, 256), :] = atth[g].astype(F32).reshape(256, 512).astype(BF)

    def home(g):
        rows = pl.ds(g * 256, 256)
        for h in range(2):
            half = pl.ds(h * 1024, 1024)
            mph[g, :, :, :, half] = nn(attm[rows, :], wom[:, half]).reshape(2, 16, 8, 1024).astype(BF)
        mixed_swap[g] = rcopy(mph.at[g, 1 - c], mrh.at[g], (sw_s, sw_r), 3 + g, sib)
        mixed_swap[g].start()

    def write(g, j, src, dst):
        copy = pltpu.make_async_copy(src.at[g], dst.at[:, g], out_l.at[2 * g + j])
        copy.start()
        written.append(copy)

    def mixed_out(g):
        wait_bytes(om.at[g, pl.ds(0, 15)], in_s.at[g])
        mixed_swap[g].wait_recv()

        @pl.loop(0, 4)
        def _(i):
            js = pl.ds(i * 4, 4)
            om[g, js] = (om[g, js].astype(F32) + (mph[g, c, js].astype(F32) + mrh[g, js].astype(F32))).astype(BF)

        write(g, 0, om, mixed)

    def grad_out(g):
        wait_bytes(gh.at[g], bk_r.at[g])

        @pl.loop(0, 4)
        def _(i):
            js = pl.ds(i * 4, 4)
            rows = pl.ds(pl.multiple_of(g * 256 + c * 128 + i * 32, 32), 32)
            gh[g, js] = (gh[g, js].astype(F32) + cotm[rows, :].astype(F32).reshape(4, 8, 2048)).astype(BF)

        write(g, 1, gh, grad)

    def w_terms(i):
        @pl.loop(0, 8)
        def _(b):
            cols = pl.ds(pl.multiple_of(b * 256, 256), 256)
            w[i, lax.div(b, 2), lax.rem(b, 2)] = tn(normed[:, cols], back[i]).reshape(4, 4, 16, 512).astype(BF)

    def o_terms():
        @pl.loop(0, 2)
        def _(b):
            cols = pl.ds(pl.multiple_of(b * 256, 256), 256)
            wo[pl.ds(2 * b, 2)] = tn(attm[:, cols], cotm[...]).reshape(2, 4, 4, 8, 2048).astype(BF)

    rs = (rs_s, rs_r)

    def term_ring(i, part, place, p):
        return RingSum(part, place, p, rs, 12 * i, via1.at[i], land1.at[i], lambda h: sum1.at[i, h])

    def term_sums(i, part2, place2, p2, place3, p3_):
        second = DirectSum(part2, place2, p2, rs, 12 * i + 6, land2.at[i], sum2.at[i])
        third = DirectSum(lambda v: sum2.at[i, :, v], place3, p3_, rs, 12 * i + 9, land3.at[i], p3.at[i])
        return second, third

    qx = term_ring(0, lambda v, h: w.at[0, v, h], at_y, y)
    qy, qz = term_sums(0, lambda v: sum1.at[0, :, v], at_z, z, at_x, x)
    kx = term_ring(1, lambda v, h: w.at[1, :, h, :, v], at_x, x)
    ky, kz = term_sums(1, lambda v: sum1.at[1, :, v], at_y, y, at_z, z)
    vx = term_ring(2, lambda v, h: w.at[2, :, h, v], at_z, z)
    vy, vz = term_sums(2, lambda v: sum1.at[2, :, :, v], at_x, x, at_y, y)
    dx = RingSum(lambda v, h: wo.at[v, pl.ds(2 * h, 2), :, :, o0], at_y, y, rs, 36, dvia, dland, lambda h: d1.at[pl.ds(2 * h, 2)])
    dy = DirectSum(lambda v: d1.at[:, v], at_x, x, rs, 42, dland2, d2)
    dz = DirectSum(lambda v: d2.at[pl.ds(v, 1)], at_z, z, rs, 45, dland3, q3.at[:, :, o0])
    ex = RingSum(lambda v, h: wo.at[pl.ds(2 * h, 2), :, v, :, o1], at_x, x, rs, 48, evia, eland, lambda h: e1.at[pl.ds(2 * h, 2)])
    ey = DirectSum(lambda v: e1.at[:, v], at_z, z, rs, 54, eland2, e2)
    ez = DirectSum(lambda v: e2.at[pl.ds(v, 1)], at_y, y, rs, 57, eland3, q3.at[:, :, o1])
    fx = RingSum(lambda v, h: wo.at[pl.ds(2 * h, 2), v, :, :, o2], at_z, z, rs, 60, fvia, fland, lambda h: f1.at[pl.ds(2 * h, 2)])
    fy = DirectSum(lambda v: f1.at[v], at_y, y, rs, 66, fland2, f2)
    fz = DirectSum(lambda v: f2.at[pl.ds(v, 1)], at_x, x, rs, 69, fland3, q3.at[:, :, o2])
    all_sums = (qx, qy, qz, kx, ky, kz, vx, vy, vz, dx, dy, dz, ex, ey, ez, fx, fy, fz)

    def gain_start(k, src):
        place, p = [(at_y, y), (at_z, z), (at_x, x)][k]
        out = []
        for d in (1, 2, 3):
            copy = rcopy(src, gland.at[3 * k + d - 1], (gn_s, gn_r), 3 * k + d - 1, place(up(p, d)))
            copy.start()
            out.append(copy)
        return out

    def gain_finish(k, src, copies):
        for copy in copies:
            copy.wait_recv()
        gacc[k] = src[...] + gland[3 * k] + gland[3 * k + 1] + gland[3 * k + 2]

    own_o.wait()
    for r in (da, ea, fa):
        r.start()
    for copy in own_w:
        copy.wait()
    for copy in swap_w:
        copy.wait_recv()
    for r in (qa, ka, va):
        r.start()
    gain[...] = gain_in[...].astype(F32).reshape(1, 2048)
    rows_i = lax.broadcasted_iota(jnp.int32, (128, 128), 0)
    cols_i = lax.broadcasted_iota(jnp.int32, (128, 128), 1)
    same = lax.rem(rows_i + 128 - cols_i, 8) == 0
    mask[...] = jnp.where(same & (cols_i <= rows_i), 0.0, -1e30)
    for a, b in ((da, db), (ea, eb), (fa, fb), (qa, qb), (ka, kb), (va, vb)):
        a.arrive()
        b.start()
    for a, b in ((db, dc), (eb, ec), (fb, fc), (qb, qc), (kb, kc), (vb, vc)):
        a.arrive()
        b.start()
    spread(0)
    cot_rows()
    for r in (dc, ec, fc):
        r.relay()
    for r in (qc, kc, vc):
        r.relay()
    for r in (dc, ec, fc):
        r.arrive()
    wo_rows()
    upstream()
    spread(1)
    pass_on(0)
    norm(0)
    qc.arrive()
    project(0, 0)
    vc.arrive()
    project(0, 2)
    kc.arrive()
    project(0, 1)
    spread(2)
    wait_bytes(upt, up_r.at[0])
    project(0, 3)
    attention(0)
    partials(0)
    pass_on(1)
    norm(1)
    for i in range(4):
        project(1, i)
    pass_on(2)
    finalize(0)
    attention(1)
    partials(1)
    norm(2)
    for i in range(4):
        project(2, i)
    finalize(1)
    attention(2)
    for r in rings:
        r.finish()
    for copy in swap_c:
        copy.wait_send()
    partials(2)
    w_terms(0)
    qx.start()
    home_rows(0)
    home_rows(1)
    w_terms(1)
    kx.start()
    home_rows(2)
    o_terms()
    for r in (dx, ex, fx):
        r.start()
    w_terms(2)
    vx.start()
    finalize(2)
    qx.relay()
    kx.relay()
    for r in (dx, ex, fx):
        r.relay()
    home(0)
    vx.relay()
    for i in range(16):
        gland[9, pl.ds(i, 1), :] = gg[:, pl.ds(128 * i, 128)]
    g0 = gain_start(0, gland.at[9])
    home(1)
    home(2)
    for a, b in ((qx, qy), (kx, ky), (dx, dy), (ex, ey), (fx, fy)):
        a.finish()
        b.start()
    gain_finish(0, gland.at[9], g0)
    g1 = gain_start(1, gacc.at[0])
    vx.finish()
    vy.start()
    mixed_out(0)
    mixed_out(1)
    mixed_out(2)
    grad_out(0)
    grad_out(1)
    for a, b in ((qy, qz), (ky, kz), (dy, dz), (ey, ez), (fy, fz)):
        a.finish()
        b.start()
    gain_finish(1, gacc.at[0], g1)
    g2 = gain_start(2, gacc.at[1])
    vy.finish()
    vz.start()
    grad_out(2)
    gain_finish(2, gacc.at[1], g2)
    g3 = rcopy(gacc.at[2], gland.at[10], (gn_s, gn_r), 9, sib)
    g3.start()
    last = {}

    def across(i):
        copy = rcopy(p3.at[i, 1 - c], p3r.at[i], (sw_s, sw_r), 6 + i, sib)
        copy.start()
        last[i] = copy

    def put(i, out):
        last[i].wait_recv()
        for j in range(4):
            cols = pl.ds(128 * j, 128)
            out[:, pl.ds(pl.multiple_of((2 * j + c) * 128, 128), 128)] = p3[i, c, :, cols]
            out[:, pl.ds(pl.multiple_of((2 * j + 1 - c) * 128, 128), 128)] = p3r[i, :, cols]

    for r in (dz, ez, fz):
        r.finish()
    for i, r in enumerate((qz, kz, vz)):
        r.finish()
        across(i)
    g_o[...] = q3[0]
    g3.wait_recv()
    gsum[...] = gacc[2] + gland[10]
    put(0, g_q)
    put(1, g_k)
    put(2, g_v)
    wait_bytes(ups.at[:, :, pl.ds(0, 15)], up_s.at[0])
    for g in range(3):
        wait_bytes(atts.at[g, :, pl.ds(0, 15)], at_s.at[g])
        wait_bytes(og.at[g, pl.ds(0, 15)], bk_s.at[g])
    for copy in written:
        copy.wait()
    for copies in (swap_w, passed.values(), swapped.values(), mixed_swap.values(), g0, g1, g2, [g3], last.values()):
        for copy in copies:
            copy.wait_send()
    for r in all_sums:
        r.drain()


def block_call(tok, cot, wq, wk, wv, w_out, gain):
    vm = pl.BlockSpec(memory_space=pltpu.VMEM)
    any_ = pl.BlockSpec(memory_space=pl.ANY)
    sds = jax.ShapeDtypeStruct
    V = pltpu.VMEM
    sem = pltpu.SemaphoreType.DMA
    rows = (16, 3, 8, 2048)
    groups = (3, 16, 8, 2048)

    def ring(lead, unit):
        return [V(lead + (4,) + unit, BF), V(lead + (2, 2) + unit, BF)]

    def out_sums(n):
        return ring((), (2, 4, 8, n)) + [V(u, BF) for u in ((4, 4, 8, n), (3, 4, 8, n), (4, 8, n), (3, 1, 8, n))]

    sems = [60, 60, 12, 12, 12, 3, 3, 3, 3, 3, 3, 1, 1, 3, 3, 9, 9, 3, 3, 72, 72, 10, 10, 7, 6]
    return pl.pallas_call(
        block_kernel,
        out_shape=(sds(rows, BF), sds(rows, BF))
        + (sds((16, 1024), F32),) * 3
        + (sds((8, 2048), F32), sds((16, 128), F32)),
        in_specs=[any_] * 6 + [vm],
        out_specs=(any_, any_) + (vm,) * 5,
        scratch_shapes=[V((2, 3, 16, 8, 2048), BF), V((3, 2, 16, 8, 2048), BF)]
        + [V((3, 4, 2, 4, 4, 16, 512), BF), V((4, 4, 4, 8, 2048), BF), V((512, 2048), BF)]
        + [V((768, 2048), BF)] * 2
        + [V((256, 2048), F32), V((4, 256, 512), BF)]
        + [V((3, 2, 16, 8, 512), BF)] * 2
        + [V((3, 768, 512), BF)]
        + [V((3, 2, 16, 8, 512), BF)] * 2
        + [V((768, 512), BF), V((128, 128), F32)]
        + [V(groups, BF), V((3, 2, 16, 8, 2048), BF)]
        + [V(groups, BF)] * 4
        + ring((3,), (4, 4, 16, 512))
        + [V((3, 2, 4, 4, 16, 512), BF)]
        + [V((3, 3, 2, 4, 16, 512), BF)]
        + [V((3, 2, 4, 16, 512), BF)]
        + [V((3, 3, 2, 16, 512), BF)]
        + [V((3, 2, 16, 512), F32), V((3, 16, 512), F32)]
        + out_sums(CUT)
        + out_sums((2048 - CUT) // 2)
        + out_sums((2048 - CUT) // 2)
        + [V((1, 8, 2048), F32)]
        + [V((1, 2048), F32), V((1, 2048), F32), V((11, 16, 128), F32), V((3, 16, 128), F32)]
        + [sem((n,)) for n in sems],
        compiler_params=pltpu.CompilerParams(collective_id=0, has_side_effects=True, vmem_limit_bytes=VMEM_LIMIT),
        name="block",
    )(tok, cot, wq, wk, wv, w_out, gain)


def finish_kernel(*refs):
    ins, outs, gsum, gain_out, held, sems = refs[:6], refs[7:13], refs[6], refs[13], refs[14:20], refs[20]
    pieces = [(i, pl.ds(4 * k, 4)) for i in range(2) for k in range(4)] + [(i, slice(None)) for i in range(2, 6)]
    enter = [pltpu.make_async_copy(ins[i].at[at], held[i].at[at], sems.at[n]) for n, (i, at) in enumerate(pieces)]
    leave = [pltpu.make_async_copy(held[i].at[at], outs[i].at[at], sems.at[12 + n]) for n, (i, at) in enumerate(pieces)]
    for copy in enter:
        copy.start()
    index = lax.axis_index("dp") * 16 + lax.axis_index("tm")
    row = gsum[pl.ds(lax.div(index, 8), 1), :]
    out = jnp.zeros((1, 16), F32)
    for i in range(8):
        out = jnp.where(lax.rem(index, 8) == i, row[:, 16 * i : 16 * i + 16], out)
    gain_out[...] = out
    for before, after in zip(enter, leave):
        before.wait()
        after.start()
    for copy in leave:
        copy.wait()


def finish_call(arrays, gsum):
    vm = pl.BlockSpec(memory_space=pltpu.VMEM)
    any_ = pl.BlockSpec(memory_space=pl.ANY)
    return pl.pallas_call(
        finish_kernel,
        out_shape=tuple(jax.ShapeDtypeStruct(a.shape, a.dtype) for a in arrays) + (jax.ShapeDtypeStruct((1, 16), F32),),
        in_specs=[any_] * 6 + [vm],
        out_specs=(any_,) * 6 + (vm,),
        scratch_shapes=[pltpu.VMEM(a.shape, a.dtype) for a in arrays] + [pltpu.SemaphoreType.DMA((24,))],
        name="finish",
    )(*arrays, gsum)


def on_device(tokens, cotangent, norm_gain, w_query, w_key, w_value, w_out):
    tok = tokens.reshape(16, 3, 8, 2048)
    cot = cotangent.reshape(16, 3, 8, 2048)
    gain = norm_gain
    *arrays, gsum = block_call(tok, cot, w_query, w_key, w_value, w_out, gain)
    mixed, grad, g_q, g_k, g_v, g_o, grad_gain = finish_call(arrays, gsum)
    shape = (1, 1, 384, 2048)
    return mixed.reshape(shape), grad.reshape(shape), grad_gain.reshape(16), g_q, g_k, g_v, g_o


def solution(mesh):
    rows = P("dp", "tm", None, None)
    weight = P(("dp", "tm"), None)
    return jax.shard_map(
        on_device,
        mesh=mesh,
        in_specs=(rows, rows, P()) + (weight,) * 4,
        out_specs=(rows, rows, P(("dp", "tm"))) + (weight,) * 4,
        check_vma=False,
    )
```
